32 devices in a mesh: gx: 4 (over z), gy: 2 (over x), gz: 4 (over y, core).
Axes of the slice: x: 2, y: 2, z: 4, core: 2. Of those that a mesh axis runs over, the one named last changes fastest.
Arguments:
- populations: float32 [19, 8, 16, 512], P(None, ('gy', 'gz'), 'gx'), may hold values from 0.5 to 1.5
- viscosity: float32 [8, 16, 512], P(('gy', 'gz'), 'gx'), may hold values from 0.01 to 0.3
- links: int32 [8, 16, 512], P(('gy', 'gz'), 'gx'), may hold values from 0 to 262143, as said below
- flags: int32 [8, 16, 512], P(('gy', 'gz'), 'gx'), may hold values from 0 to 2, as said below
- neighbours: int32 [8, 16, 18], P(('gy', 'gz'), 'gx'), may hold values from -1 to 15, as said below
- owners: int32 [8, 16], P(('gy', 'gz')), may hold values from 0 to 3, as said below
- slots: int32 [8, 16], P(('gy', 'gz')), may hold values from 0 to 15, as said below
- concentrations: float32 [4, 32, 16, 512], P(None, 'gx', 'gy', 'gz'), may hold values from 0.2 to 2
- diffusivity: float32 [32, 16, 512], P('gx', 'gy', 'gz'), may hold values from 0.04 to 0.12
- uptake_rate: float32 [32, 16, 512], P('gx', 'gy', 'gz'), may hold values from 0.02 to 0.2
Outputs:
- weighted_populations: float32 [19, 8, 16, 512], P(None, ('gy', 'gz'), 'gx')
- tissue_conc: float32 [4, 32, 16, 512], P(None, 'gx', 'gy', 'gz')
The draws below stay inside these ranges and needn't reach their ends.
Inputs may be any that keep to these rules, and one draw needn't show every extreme that they name: `links`: bit i - 1 is set when the link of population i into the site is open. `flags`: 0 interior site, 1 inlet site, 2 outlet site. `neighbours`: -1 where no block lies beside; the relation is mutual: if block b has N in direction k, N has b in the opposite direction; a block beside lies in the list of the same index of gx or of the one next to it. `owners`: no two of the 4 blocks on one index of gx have the same owner, and in every segment some owner receives exactly 1 from every index of gx. `slots`: distinct among the blocks of one segment with one owner.
All inputs are finite; a program needn't handle non-finite values.
Results may differ from the reference program's by a relative error of at most 0.0003.
Values sent between devices are 32-bit elements; how exact they have to be, the bound alone decides.
A program may use at most 128 MiB of HBM per device.

```python
import math
import jax
import jax.numpy as jnp
import numpy as np
from jax import lax

Q = 19
SITES = 512
SPECIES = 4
FLOW_STEPS = 4
TISSUE_STEPS = 3
BLK_DEV = 4
BX = 8
BY = 8
BZ = 128
CAP = 1
OWNERS = 4
SEGS = 8
SEG_BLOCKS = 16
BRICK_SLOTS = 16
NX = 32
NY = 16
NZ = 512
N_GZ = 4


MOVING_DIRS = ((1, 0, 0), (-1, 0, 0), (0, 1, 0), (0, -1, 0), (0, 0, 1), (0, 0, -1), (1, 1, 0), (-1, -1, 0), (1, -1, 0), (-1, 1, 0), (1, 0, 1), (-1, 0, -1), (1, 0, -1), (-1, 0, 1), (0, 1, 1), (0, -1, -1), (0, 1, -1), (0, -1, 1))


def vessel_layout(key):
    base_key = jax.random.fold_in(key, 11)
    length = SEG_BLOCKS // 4
    vectors = jnp.array(MOVING_DIRS, jnp.int32)

    def one_segment(seg_key):
        local_perm = jax.vmap(lambda row_key: jax.random.permutation(row_key, BLK_DEV))(jax.random.split(seg_key, OWNERS)).astype(jnp.int32)
        order = (jnp.arange(OWNERS, dtype=jnp.int32)[:, None] * BLK_DEV + local_perm).reshape(SEG_BLOCKS)
        inverse = jnp.zeros((SEG_BLOCKS,), jnp.int32).at[order].set(jnp.arange(SEG_BLOCKS, dtype=jnp.int32))
        pos_z = order // 4
        pos_x = order % 4 // 2
        pos_y = order % 2
        target_x = pos_x[:, None] + vectors[None, :, 0]
        target_y = pos_y[:, None] + vectors[None, :, 1]
        target_z = pos_z[:, None] + vectors[None, :, 2]
        inside = (target_x >= 0) & (target_x < 2) & (target_y >= 0) & (target_y < 2) & (target_z >= 0) & (target_z < length)
        target = target_z * 4 + target_x * 2 + target_y
        beside = jnp.where(inside, inverse[jnp.clip(target, 0, SEG_BLOCKS - 1)], -1)
        third = jnp.arange(SITES, dtype=jnp.int32) % 8
        kinds = jnp.where((pos_z[:, None] == 0) & (third[None, :] == 0), 1, 0)
        kinds = jnp.where((pos_z[:, None] == length - 1) & (third[None, :] == 7), 2, kinds)
        flipped = jax.random.randint(jax.random.fold_in(seg_key, 5), (), 0, 2)
        kinds = jnp.where((kinds > 0) & (flipped == 1), 3 - kinds, kinds)
        return (beside.astype(jnp.int32), kinds.astype(jnp.int32))
    return jax.vmap(one_segment)(jax.random.split(base_key, SEGS))


def owner_layout(key):
    base_key = jax.random.fold_in(key, 31)

    def one_segment(seg_key):
        key_hot, key_turn, key_order, key_slot = jax.random.split(seg_key, 4)
        hottest = jax.random.randint(key_hot, (), 0, OWNERS)
        turns = jax.random.randint(key_turn, (OWNERS, 1), 0, OWNERS - 1)
        column = jnp.arange(BLK_DEV, dtype=jnp.int32)[None, :]
        spread_owner = (hottest + 1 + (turns + column - CAP) % (OWNERS - 1)) % OWNERS
        base_rows = jnp.where(column < CAP, hottest, spread_owner)
        orders = jax.vmap(lambda row_key: jax.random.permutation(row_key, BLK_DEV))(jax.random.split(key_order, OWNERS))
        owner_row = jnp.take_along_axis(base_rows, orders.astype(jnp.int32), axis=1).reshape(SEG_BLOCKS).astype(jnp.int32)
        matches = (owner_row[:, None] == jnp.arange(OWNERS, dtype=jnp.int32)[None, :]).astype(jnp.int32)
        ranks = jnp.sum(matches * (jnp.cumsum(matches, axis=0) - 1), axis=1)
        slot_perms = jax.vmap(lambda row_key: jax.random.permutation(row_key, BRICK_SLOTS))(jax.random.split(key_slot, OWNERS)).astype(jnp.int32)
        slot_perms = (slot_perms - slot_perms[:, :1] + BRICK_SLOTS - 1) % BRICK_SLOTS
        slot_row = slot_perms[owner_row, ranks]
        return (owner_row, slot_row.astype(jnp.int32))
    return jax.vmap(one_segment)(jax.random.split(base_key, SEGS))


def draw_links(key, part):
    bits_key = jax.random.fold_in(key, 23)
    raw = jax.random.randint(bits_key, (SEGS, SEG_BLOCKS, SITES, 18), 0, 8)
    opened = (raw != 0).astype(jnp.int32)
    powers = jnp.left_shift(jnp.ones((18,), jnp.int32), jnp.arange(18, dtype=jnp.int32))
    return jnp.sum(opened * powers, axis=-1).astype(jnp.int32)


def draw_flags(key, part):
    return vessel_layout(key)[1]


def draw_neighbours(key, part):
    return vessel_layout(key)[0]


def draw_owners(key, part):
    return owner_layout(key)[0]


def draw_slots(key, part):
    return owner_layout(key)[1]


def levels(own_key, dims, cuts, least, largest):
    def one(axis_at, blocks):
        steps = jax.random.uniform(jax.random.fold_in(jax.random.fold_in(own_key, 6), axis_at), (blocks,), jnp.float32, least / len(cuts), largest / len(cuts))
        return jnp.repeat(jnp.exp(steps), dims[axis_at] // blocks).reshape((-1,) + (1,) * (len(dims) - axis_at - 1))

    factor_of = one(*cuts[0])
    for cut in cuts[1:]:
        factor_of = factor_of * one(*cut)
    return factor_of


def setup_inputs(seed: int = 0) -> dict:
    streams_of = jax.random.split(jax.random.key(seed), 11)
    return {
        "populations": jnp.clip(0.5 + 1.0 * jax.random.uniform(streams_of[0], (Q, SEGS, SEG_BLOCKS, SITES), jnp.float32) ** levels(streams_of[0], (Q, SEGS, SEG_BLOCKS, SITES), ((1, 8), (2, 4)), -0.2, 0.2), 0.5, 1.5),
        "viscosity": jnp.clip(jnp.exp(math.log(0.3) - 3.4011974 * jax.random.uniform(streams_of[1], (SEGS, SEG_BLOCKS, SITES), jnp.float32) ** levels(streams_of[1], (SEGS, SEG_BLOCKS, SITES), ((0, 8), (1, 4)), -0.2, 0.2)), 0.01, 0.3),
        "links": draw_links(jax.random.fold_in(streams_of[10], 71), 0),
        "flags": draw_flags(jax.random.fold_in(streams_of[10], 71), 0),
        "neighbours": draw_neighbours(jax.random.fold_in(streams_of[10], 71), 0),
        "owners": draw_owners(jax.random.fold_in(streams_of[10], 71), 0),
        "slots": draw_slots(jax.random.fold_in(streams_of[10], 71), 0),
        "concentrations": jnp.clip(0.2 + 1.8 * jax.random.uniform(streams_of[7], (SPECIES, NX, NY, NZ), jnp.float32) ** levels(streams_of[7], (SPECIES, NX, NY, NZ), ((1, 4), (2, 2), (3, 4)), -0.2, 0.2), 0.2, 2.0),
        "diffusivity": jnp.clip(jnp.exp(math.log(0.12) - 1.0986123 * jax.random.uniform(streams_of[8], (NX, NY, NZ), jnp.float32) ** levels(streams_of[8], (NX, NY, NZ), ((0, 4), (1, 2), (2, 4)), -0.2, 0.2)), 0.04, 0.12),
        "uptake_rate": jnp.clip(jnp.exp(math.log(0.2) - 2.3025851 * jax.random.uniform(streams_of[9], (NX, NY, NZ), jnp.float32) ** levels(streams_of[9], (NX, NY, NZ), ((0, 4), (1, 2), (2, 4)), -0.2, 0.2)), 0.02, 0.2),
    }


LATTICE_DIRS = ((0, 0, 0), (1, 0, 0), (-1, 0, 0), (0, 1, 0), (0, -1, 0), (0, 0, 1), (0, 0, -1), (1, 1, 0), (-1, -1, 0), (1, -1, 0), (-1, 1, 0), (1, 0, 1), (-1, 0, -1), (1, 0, -1), (-1, 0, 1), (0, 1, 1), (0, -1, -1), (0, 1, -1), (0, -1, 1))
DIFFUSION_GAIN = (1.0, 0.6, 0.7, 0.35)
HALF_SATURATION = (0.3, 0.5, 0.8, 0.2)
ADVECT_GAIN = 3.0
INLET_DENSITY = 1.03
OUTLET_DENSITY = 0.97


def lattice_tables(shell):
    vectors = np.array(LATTICE_DIRS, dtype=np.int64)
    weights = np.array([1.0 / 3.0] + [1.0 / 18.0] * 6 + [1.0 / 36.0] * 12)
    opposite = [LATTICE_DIRS.index(tuple(-part_val for part_val in LATTICE_DIRS[member])) for member in range(19)]
    sites = np.arange(512)
    coords = np.stack([sites // 64, (sites // 8) % 8, sites % 8], axis=1)
    stride = np.array([64, 8, 1])
    shell_sites = sites[((coords == 0) | (coords == 7)).any(axis=1)]
    position = {}
    rim_source = []
    for member in range(1, 19):
        moved = coords + vectors[member]
        leaving = ((moved < 0) | (moved > 7)).any(axis=1)
        chosen = shell_sites if shell else sites[leaving]
        for site_id in chosen:
            position[(member, int(site_id))] = len(rim_source)
            rim_source.append(member * 512 + int(site_id))
    rim_width = -(-len(rim_source) // 128) * 128
    request_dir = []
    request_pos = []
    offsets = [0]
    counts = [0]
    selects = [sites.copy()]
    dir_maps = [np.zeros(512, np.int64)]
    arriving_masks = [np.zeros(512, bool)]
    shifts = [0]
    for member in range(1, 19):
        source = coords - vectors[member]
        arriving = ((source < 0) | (source > 7)).any(axis=1)
        select = sites.copy()
        dir_map = np.zeros(512, np.int64)
        offsets.append(len(request_dir))
        counts.append(int(arriving.sum()))
        for rank_pos, site_id in enumerate(sites[arriving]):
            block_dir = tuple(int(part_val) for part_val in (source[site_id] // 8))
            dir_index = LATTICE_DIRS.index(block_dir) - 1
            local_site = int(((source[site_id] % 8) * stride).sum())
            request_dir.append(dir_index)
            request_pos.append(position[(member, local_site)])
            select[site_id] = 512 + rank_pos
            dir_map[site_id] = dir_index
        selects.append(select)
        dir_maps.append(dir_map)
        arriving_masks.append(arriving)
        shifts.append(int((vectors[member] * stride).sum()))
    request_width = -(-len(request_dir) // 128) * 128
    request_dir = request_dir + [0] * (request_width - len(request_dir))
    request_pos = request_pos + [0] * (request_width - len(request_pos))
    return {"vectors": vectors, "weights": weights, "opposite": opposite, "rim_source": np.array(rim_source), "rim_width": rim_width, "request_dir": np.array(request_dir), "request_pos": np.array(request_pos), "offsets": offsets, "counts": counts, "selects": selects, "dir_maps": dir_maps, "arriving": arriving_masks, "shifts": shifts}


def equilibrium(density, momentum, vectors, weights):
    project = jnp.tensordot(vectors, momentum, axes=1, precision=lax.Precision.HIGHEST)
    square = jnp.sum(momentum * momentum, axis=0)
    return weights[:, None, None] * (density + 3.0 * project + 4.5 * project * project - 1.5 * square)


def collide(popul, relax, vectors, weights):
    density = jnp.sum(popul, axis=0)
    momentum = jnp.tensordot(vectors.T, popul, axes=1, precision=lax.Precision.HIGHEST)
    return popul - relax * (popul - equilibrium(density, momentum, vectors, weights))


def rim_rows(post, tables):
    block_count = post.shape[1]
    flat = jnp.transpose(post, (1, 0, 2)).reshape(block_count, 19 * 512)
    rim = jnp.take(flat, jnp.asarray(tables["rim_source"], jnp.int32), axis=1)
    return jnp.pad(rim, ((0, 0), (0, tables["rim_width"] - rim.shape[1])))


def stream(post, arrived, link_bits, beside_ids, tables):
    result = [post[0]]
    for member in range(1, 19):
        rolled = jnp.roll(post[member], tables["shifts"][member], axis=-1)
        start_col = tables["offsets"][member]
        pool = jnp.concatenate([rolled, arrived[:, start_col:start_col + tables["counts"][member]]], axis=1)
        pulled = jnp.take(pool, jnp.asarray(tables["selects"][member], jnp.int32), axis=1)
        beside = jnp.take(beside_ids, jnp.asarray(tables["dir_maps"][member], jnp.int32), axis=1) >= 0
        link_open = jnp.right_shift(link_bits, member - 1) % 2 == 1
        arriving = jnp.asarray(tables["arriving"][member])[None, :]
        opened = link_open & (beside | jnp.logical_not(arriving))
        result.append(jnp.where(opened, pulled, post[tables["opposite"][member]]))
    return jnp.stack(result)


def boundary(popul, site_flags, vectors, weights):
    momentum = jnp.tensordot(vectors.T, popul, axes=1, precision=lax.Precision.HIGHEST)
    density = jnp.where(site_flags == 1, INLET_DENSITY, OUTLET_DENSITY)
    settled = equilibrium(density, momentum, vectors, weights)
    return jnp.where(site_flags[None] > 0, settled, popul)


def shifted(field, offset):
    extent_x, extent_y, extent_z = field.shape[-3:]
    step_x, step_y, step_z = offset
    return field[..., 1 + step_x:extent_x - 1 + step_x, 1 + step_y:extent_y - 1 + step_y, 1 + step_z:extent_z - 1 + step_z]


def tissue_step(conc_ext, diff_ext, uptake_here, velocity):
    center = conc_ext[:, 1:-1, 1:-1, 1:-1]
    diff_mid = diff_ext[1:-1, 1:-1, 1:-1]
    spread = jnp.zeros_like(center)
    for offset in ((1, 0, 0), (-1, 0, 0), (0, 1, 0), (0, -1, 0), (0, 0, 1), (0, 0, -1)):
        beside_conc = shifted(conc_ext, offset)
        beside_diff = shifted(diff_ext, offset)
        spread = spread + 0.5 * (diff_mid + beside_diff) * (beside_conc - center)
    drifted = jnp.zeros_like(center)
    for axis_pos in range(3):
        unit_vec = [0, 0, 0]
        unit_vec[axis_pos] = 1
        ahead = shifted(conc_ext, tuple(unit_vec))
        behind = shifted(conc_ext, tuple(-part_val for part_val in unit_vec))
        speed_axis = ADVECT_GAIN * velocity[axis_pos]
        drifted = drifted - jnp.maximum(speed_axis, 0.0) * (center - behind) - jnp.minimum(speed_axis, 0.0) * (ahead - center)
    species_gain = jnp.array(DIFFUSION_GAIN, jnp.float32)[:, None, None, None]
    halfsat = jnp.array(HALF_SATURATION, jnp.float32)[:, None, None, None]
    uptake = uptake_here * center / (halfsat + jnp.abs(center))
    reaction = jnp.stack([-uptake[0], -uptake[1], 2.0 * uptake[1], -uptake[3]])
    return center + species_gain * spread + drifted + reaction


def reference(populations, viscosity, links, flags, neighbours, owners, slots, concentrations, diffusivity, uptake_rate):
    tables = lattice_tables(False)
    weights = jnp.asarray(tables["weights"], jnp.float32)
    vectors = jnp.asarray(tables["vectors"], jnp.float32)
    request_dir = jnp.asarray(tables["request_dir"], jnp.int32)
    request_pos = jnp.asarray(tables["request_pos"], jnp.int32)

    def segment(operands):
        pops_seg, visc_seg, link_seg, flag_seg, beside_seg = operands
        popul = pops_seg * weights[:, None, None]
        relax = 1.0 / (3.0 * visc_seg + 0.5)
        block_count = popul.shape[1]
        request_block = jnp.take(beside_seg, request_dir, axis=1)
        for turn_index in range(FLOW_STEPS):
            post = collide(popul, relax, vectors, weights)
            rim = rim_rows(post, tables)
            flat_index = jnp.clip(request_block, 0, block_count - 1) * rim.shape[1] + request_pos[None, :]
            arrived = jnp.take(rim.reshape(-1), flat_index)
            popul = stream(post, arrived, link_seg, beside_seg, tables)
            popul = boundary(popul, flag_seg, vectors, weights)
        momentum = jnp.tensordot(vectors.T, popul, axes=1, precision=lax.Precision.HIGHEST)
        return popul / weights[:, None, None], momentum

    weighted, momentum = lax.map(segment, (jnp.moveaxis(populations, 1, 0), viscosity, links, flags, neighbours))
    weighted = jnp.moveaxis(weighted, 0, 1)
    slot_x = BX // 8
    slot_y = BY // 8
    slot_z = BZ // 8
    seg_ids = jnp.arange(SEGS, dtype=jnp.int32)
    row_y = seg_ids // N_GZ
    row_z = seg_ids % N_GZ
    place_x = owners * slot_x + slots // (slot_y * slot_z)
    place_y = row_y[:, None] * slot_y + (slots // slot_z) % slot_y
    place_z = row_z[:, None] * slot_z + slots % slot_z
    values = jnp.transpose(momentum, (0, 2, 1, 3)).reshape(SEGS * SEG_BLOCKS, 3, 512)
    grid = jnp.zeros((NX // 8, NY // 8, NZ // 8, 3, 512), jnp.float32)
    grid = grid.at[place_x.reshape(-1), place_y.reshape(-1), place_z.reshape(-1)].set(values)
    velocity = grid.reshape(NX // 8, NY // 8, NZ // 8, 3, 8, 8, 8).transpose(3, 0, 4, 1, 5, 2, 6).reshape(3, NX, NY, NZ)
    diff_ext = jnp.pad(diffusivity, 1)
    conc = concentrations
    for turn_index in range(TISSUE_STEPS):
        conc_ext = jnp.pad(conc, ((0, 0), (1, 1), (1, 1), (1, 1)))
        conc = tissue_step(conc_ext, diff_ext, uptake_rate, velocity)
    return weighted, conc
```

```python
import jax
import jax.numpy as jnp
import numpy as np
from jax import lax
from jax.experimental import pallas as pl
from jax.experimental.pallas import tpu as pltpu
from jax.sharding import PartitionSpec as P

FLOW_STEPS = 4
TISSUE_STEPS = 3


LATTICE_DIRS = (
    (0, 0, 0),
    (1, 0, 0),
    (-1, 0, 0),
    (0, 1, 0),
    (0, -1, 0),
    (0, 0, 1),
    (0, 0, -1),
    (1, 1, 0),
    (-1, -1, 0),
    (1, -1, 0),
    (-1, 1, 0),
    (1, 0, 1),
    (-1, 0, -1),
    (1, 0, -1),
    (-1, 0, 1),
    (0, 1, 1),
    (0, -1, -1),
    (0, 1, -1),
    (0, -1, 1),
)
DIFFUSION_GAIN = (1.0, 0.6, 0.7, 0.35)
HALF_SATURATION = (0.3, 0.5, 0.8, 0.2)
ADVECT_GAIN = 3.0
INLET_DENSITY = 1.03
OUTLET_DENSITY = 0.97


def padded(cells, sides, width):
    for axis, dim in sides:
        count = lax.axis_size(axis)
        ends = count - 1
        head = lax.slice_in_dim(cells, 0, width, axis=dim)
        tail = lax.slice_in_dim(cells, cells.shape[dim] - width, cells.shape[dim], axis=dim)
        cells = jnp.concatenate(
            [
                lax.ppermute(tail, axis, [(i, (i + 1) % count) for i in range(ends)]),
                cells,
                lax.ppermute(head, axis, [((i + 1) % count, i) for i in range(ends)]),
            ],
            axis=dim,
        )
    return cells


def lattice_tables():
    vectors = np.array(LATTICE_DIRS, dtype=np.int64)
    weights = np.array([1.0 / 3.0] + [1.0 / 18.0] * 6 + [1.0 / 36.0] * 12)
    opposite = [
        LATTICE_DIRS.index(tuple((-part_val for part_val in LATTICE_DIRS[member])))
        for member in range(19)
    ]
    sites = np.arange(512)
    coords = np.stack([sites // 64, sites // 8 % 8, sites % 8], axis=1)
    stride = np.array([64, 8, 1])
    position = {}
    rim_source = []
    for member in range(1, 19):
        moved = coords + vectors[member]
        leaving = ((moved < 0) | (moved > 7)).any(axis=1)
        chosen = sites[leaving]
        for site_id in chosen:
            position[member, int(site_id)] = len(rim_source)
            rim_source.append(member * 512 + int(site_id))
    rim_width = -(-len(rim_source) // 128) * 128
    request_dir = []
    request_pos = []
    offsets = [0]
    counts = [0]
    selects = [sites.copy()]
    dir_maps = [np.zeros(512, np.int64)]
    arriving_masks = [np.zeros(512, bool)]
    shifts = [0]
    for member in range(1, 19):
        source = coords - vectors[member]
        arriving = ((source < 0) | (source > 7)).any(axis=1)
        select = sites.copy()
        dir_map = np.zeros(512, np.int64)
        offsets.append(len(request_dir))
        counts.append(int(arriving.sum()))
        for rank_pos, site_id in enumerate(sites[arriving]):
            block_dir = tuple((int(part_val) for part_val in source[site_id] // 8))
            dir_index = LATTICE_DIRS.index(block_dir) - 1
            local_site = int((source[site_id] % 8 * stride).sum())
            request_dir.append(dir_index)
            request_pos.append(position[member, local_site])
            select[site_id] = 512 + rank_pos
            dir_map[site_id] = dir_index
        selects.append(select)
        dir_maps.append(dir_map)
        arriving_masks.append(arriving)
        shifts.append(int((vectors[member] * stride).sum()))
    request_width = -(-len(request_dir) // 128) * 128
    request_dir = request_dir + [0] * (request_width - len(request_dir))
    request_pos = request_pos + [0] * (request_width - len(request_pos))
    return {
        "vectors": vectors,
        "weights": weights,
        "opposite": opposite,
        "rim_source": np.array(rim_source),
        "rim_width": rim_width,
        "request_dir": np.array(request_dir),
        "request_pos": np.array(request_pos),
        "offsets": offsets,
        "counts": counts,
        "selects": selects,
        "dir_maps": dir_maps,
        "arriving": arriving_masks,
        "shifts": shifts,
    }


def equilibrium(density, momentum, vectors, weights):
    project = jnp.tensordot(vectors, momentum, axes=1, precision=lax.Precision.HIGHEST)
    square = jnp.sum(momentum * momentum, axis=0)
    return weights[:, None, None] * (
        density + 3.0 * project + 4.5 * project * project - 1.5 * square
    )


def collide(popul, relax, vectors, weights):
    density = jnp.sum(popul, axis=0)
    momentum = jnp.tensordot(vectors.T, popul, axes=1, precision=lax.Precision.HIGHEST)
    return popul - relax * (popul - equilibrium(density, momentum, vectors, weights))


def rim_rows(post, tables):
    block_count = post.shape[1]
    flat = jnp.transpose(post, (1, 0, 2)).reshape(block_count, 19 * 512)
    rim = jnp.take(flat, jnp.asarray(tables["rim_source"], jnp.int32), axis=1)
    return jnp.pad(rim, ((0, 0), (0, tables["rim_width"] - rim.shape[1])))


def stream(post, arrived, link_bits, beside_ids, tables):
    result = [post[0]]
    for member in range(1, 19):
        rolled = jnp.roll(post[member], tables["shifts"][member], axis=-1)
        start_col = tables["offsets"][member]
        pool = jnp.concatenate(
            [rolled, arrived[:, start_col : start_col + tables["counts"][member]]], axis=1
        )
        pulled = jnp.take(pool, jnp.asarray(tables["selects"][member], jnp.int32), axis=1)
        beside = (
            jnp.take(beside_ids, jnp.asarray(tables["dir_maps"][member], jnp.int32), axis=1) >= 0
        )
        link_open = jnp.right_shift(link_bits, member - 1) % 2 == 1
        arriving = jnp.asarray(tables["arriving"][member])[None, :]
        opened = link_open & (beside | jnp.logical_not(arriving))
        result.append(jnp.where(opened, pulled, post[tables["opposite"][member]]))
    return jnp.stack(result)


def boundary(popul, site_flags, vectors, weights):
    momentum = jnp.tensordot(vectors.T, popul, axes=1, precision=lax.Precision.HIGHEST)
    density = jnp.where(site_flags == 1, INLET_DENSITY, OUTLET_DENSITY)
    settled = equilibrium(density, momentum, vectors, weights)
    return jnp.where(site_flags[None] > 0, settled, popul)


def shifted(field, offset):
    extent_x, extent_y, extent_z = field.shape[-3:]
    step_x, step_y, step_z = offset
    return field[
        ...,
        1 + step_x : extent_x - 1 + step_x,
        1 + step_y : extent_y - 1 + step_y,
        1 + step_z : extent_z - 1 + step_z,
    ]


def tissue_step(conc_ext, diff_ext, uptake_here, velocity):
    center = conc_ext[:, 1:-1, 1:-1, 1:-1]
    diff_mid = diff_ext[1:-1, 1:-1, 1:-1]
    spread = jnp.zeros_like(center)
    for offset in ((1, 0, 0), (-1, 0, 0), (0, 1, 0), (0, -1, 0), (0, 0, 1), (0, 0, -1)):
        beside_conc = shifted(conc_ext, offset)
        beside_diff = shifted(diff_ext, offset)
        spread = spread + 0.5 * (diff_mid + beside_diff) * (beside_conc - center)
    drifted = jnp.zeros_like(center)
    for axis_pos in range(3):
        unit_vec = [0, 0, 0]
        unit_vec[axis_pos] = 1
        ahead = shifted(conc_ext, tuple(unit_vec))
        behind = shifted(conc_ext, tuple((-part_val for part_val in unit_vec)))
        speed_axis = ADVECT_GAIN * velocity[axis_pos]
        drifted = (
            drifted
            - jnp.maximum(speed_axis, 0.0) * (center - behind)
            - jnp.minimum(speed_axis, 0.0) * (ahead - center)
        )
    species_gain = jnp.array(DIFFUSION_GAIN, jnp.float32)[:, None, None, None]
    halfsat = jnp.array(HALF_SATURATION, jnp.float32)[:, None, None, None]
    uptake = uptake_here * center / (halfsat + jnp.abs(center))
    reaction = jnp.stack([-uptake[0], -uptake[1], 2.0 * uptake[1], -uptake[3]])
    return center + species_gain * spread + drifted + reaction


def shards(
    populations,
    viscosity,
    links,
    flags,
    neighbours,
    owners,
    slots,
    concentrations,
    diffusivity,
    uptake_rate,
):
    tables = lattice_tables()
    weights = jnp.asarray(tables["weights"], jnp.float32)
    vectors = jnp.asarray(tables["vectors"], jnp.float32)
    popul = populations[:, 0] * weights[:, None, None]
    relax = 1.0 / (3.0 * viscosity[0] + 0.5)
    link_bits = links[0]
    site_flags = flags[0]
    beside_ids = neighbours[0]
    block_count = popul.shape[1]
    request_block = jnp.take(beside_ids, jnp.asarray(tables["request_dir"], jnp.int32), axis=1)
    request_pos = jnp.asarray(tables["request_pos"], jnp.int32)
    first_block = (lax.axis_index("gx") - 1) * block_count
    local_block = request_block - first_block
    valid = (local_block >= 0) & (local_block < 3 * block_count)
    for turn_index in range(FLOW_STEPS):
        post = collide(popul, relax, vectors, weights)
        rim = rim_rows(post, tables)
        extended = padded(rim, (("gx", 0),), block_count)
        flat_index = (
            jnp.clip(local_block, 0, 3 * block_count - 1) * extended.shape[1] + request_pos[None, :]
        )
        arrived = jnp.where(valid, jnp.take(extended.reshape(-1), flat_index), 0.0)
        popul = stream(post, arrived, link_bits, beside_ids, tables)
        popul = boundary(popul, site_flags, vectors, weights)
    weighted = (popul / weights[:, None, None])[:, None]
    momentum = jnp.tensordot(vectors.T, popul, axes=1, precision=lax.Precision.HIGHEST)
    block_rows = jnp.transpose(momentum, (1, 0, 2)).reshape(block_count, 3 * 512)
    extent_x, extent_y, extent_z = concentrations.shape[1:]
    slot_x = extent_x // 8
    slot_y = extent_y // 8
    slot_z = extent_z // 8
    slot_total = slot_x * slot_y * slot_z
    owner_all = owners[0]
    slot_all = slots[0]
    my_index = lax.axis_index("gx")
    slot_ids = jnp.arange(slot_total, dtype=jnp.int32)
    start_blocks = jnp.zeros((slot_total, 3 * 512), jnp.float32)
    piece = jax.tree.map(lambda part: lax.all_gather(part, "gx", axis=0, tiled=True), block_rows)
    row_count = piece.shape[0]
    piece_owner = lax.slice_in_dim(owner_all, 0, row_count, axis=0)
    piece_slot = lax.slice_in_dim(slot_all, 0, row_count, axis=0)
    hit = (piece_owner[None, :] == my_index) & (piece_slot[None, :] == slot_ids[:, None])
    brick_blocks = start_blocks + jnp.dot(
        hit.astype(jnp.float32), piece, precision=lax.Precision.HIGHEST
    )
    velocity = (
        brick_blocks.reshape(slot_x, slot_y, slot_z, 3, 8, 8, 8)
        .transpose(3, 0, 4, 1, 5, 2, 6)
        .reshape(3, extent_x, extent_y, extent_z)
    )
    conc_ext, diff_ext = (
        padded(concentrations, (("gx", 1), ("gy", 2), ("gz", 3)), 1),
        padded(diffusivity[None], (("gx", 1), ("gy", 2), ("gz", 3)), 1),
    )
    diff_ext = diff_ext[0]
    conc = tissue_step(conc_ext, diff_ext, uptake_rate, velocity)
    for turn_index in range(TISSUE_STEPS - 1):
        conc_ext = padded(conc, (("gx", 1), ("gy", 2), ("gz", 3)), 1)
        conc = tissue_step(conc_ext, diff_ext, uptake_rate, velocity)
    return (weighted, conc)


MESH = pl.DeviceIdType.MESH
AXES = ("gx", "gy", "gz")
CHUNKS = 2


def iota(axis):
    return lax.broadcasted_iota(jnp.int32, (8, 128), axis)


def take(values, index, axis):
    return jnp.take_along_axis(values, index, axis=axis, mode="promise_in_bounds")


def swap_indices():
    row, lane = iota(0), iota(1)
    half, group, cell = lane // 64, (lane // 8) % 8, lane % 8
    ahead = half * 64 + ((group + row) % 8) * 8 + cell
    rows = (row - group + 8) % 8
    back = half * 64 + rows * 8 + cell
    return ahead, rows, back


def swap(values, indices):
    ahead, rows, back = indices
    return take(take(take(values, ahead, 1), rows, 0), back, 1)


def tables_needed():
    keys = []
    for vec in LATTICE_DIRS[1:]:
        for face_x in {0, -vec[0]}:
            for face_y in {0, -vec[1]}:
                key = (face_x, face_y, vec[2])
                if key != (0, 0, 0) and key not in keys:
                    keys.append(key)
    return sorted(keys)


TABLE_KEYS = tables_needed()


def weight_of(member):
    return 1.0 / 3.0 if member == 0 else (1.0 / 18.0 if member < 7 else 1.0 / 36.0)


def moments(popul):
    density = popul[0]
    momentum = [None, None, None]
    for member in range(1, 19):
        density = density + popul[member]
        for axis in range(3):
            sign = LATTICE_DIRS[member][axis]
            if sign:
                term = popul[member]
                if momentum[axis] is None:
                    momentum[axis] = term if sign > 0 else -term
                else:
                    momentum[axis] = momentum[axis] + term if sign > 0 else momentum[axis] - term
    return density, momentum


def relaxed(popul, density, momentum, relax):
    square = momentum[0] * momentum[0] + momentum[1] * momentum[1] + momentum[2] * momentum[2]
    rest = density - 1.5 * square
    result = [popul[0] - relax * (popul[0] - rest * (1.0 / 3.0))]
    for member in range(1, 19, 2):
        vec = LATTICE_DIRS[member]
        weight = weight_of(member)
        project = None
        for axis in range(3):
            if vec[axis]:
                term = momentum[axis]
                if project is None:
                    project = term if vec[axis] > 0 else -term
                else:
                    project = project + term if vec[axis] > 0 else project - term
        even = weight * rest + (4.5 * weight) * (project * project)
        odd = (3.0 * weight) * project
        result.append(popul[member] - relax * (popul[member] - (even + odd)))
        result.append(popul[member + 1] - relax * (popul[member + 1] - (even - odd)))
    return result


def sides_of(axis):
    count = lax.axis_size(axis)
    here = lax.axis_index(axis)
    return (
        (here > 0, {axis: lax.max(here - 1, 0)}),
        (here < count - 1, {axis: lax.min(here + 1, count - 1)}),
    )


def kernel(
    pops, visc, links, flags, beside, owners, slots, conc, diff, uptake,
    weighted, conc_out,
    gathered, fields, post, tables, open_bits, relax_by, marks,
    cells, rates, winds, halo_x, halo_y, halo_z, pack_y, pack_z,
    send_g, recv_g, send_t, recv_t,
):
    count = lax.axis_size("gx")
    here = lax.axis_index("gx")
    block_count = pops.shape[1]
    species = conc.shape[0]
    planes = gathered.shape[1]
    lane, row = iota(1), iota(0)
    block_lane, cell_lane = lane // 8, lane % 8
    halos = (halo_x, halo_y, halo_z)

    for at, axis in enumerate(AXES):
        for side, (there, _) in enumerate(sides_of(axis)):

            @pl.when(jnp.logical_not(there))
            def _(at=at, side=side):
                for turn in range(TISSUE_STEPS):
                    halos[at][turn, side] = jnp.zeros(halos[at].shape[2:], jnp.float32)

    gathered[here, 0:19] = pops[...]
    gathered[here, 19] = visc[...]
    gathered[here, 20] = links[...].astype(jnp.float32)
    gathered[here, 21] = flags[...].astype(jnp.float32)
    gathered[here, 22] = jnp.zeros((block_count, 512), jnp.float32)
    gathered[here, 22, :, 0:18] = beside[...].astype(jnp.float32)
    for kind in range(species):
        cells[0, kind] = conc[kind]
    cells[0, species] = diff[...]

    def pack(slot, turn):
        kinds = species + 1 if turn == 0 else species
        for side, spot in ((0, 0), (1, 7)):
            zcol = 0 if side == 0 else 127
            packed = jnp.zeros((8, 128), jnp.float32)
            for kind in range(kinds):
                for a in range(8):
                    tile = cells[slot, kind, a]
                    pack_y[turn, side, kind, a : a + 1] = tile[spot : spot + 1]
                    packed = jnp.where(
                        lane == kind * 8 + a,
                        jnp.broadcast_to(tile[:, zcol : zcol + 1], (8, 128)),
                        packed,
                    )
            pack_z[turn, side] = packed

    def face_copy(slot, turn, at, side, device, landing):
        kinds = species + 1 if turn == 0 else species
        if at == 0:
            source = cells.at[slot, pl.ds(0, kinds), 0 if side == 0 else 7]
            target = halo_x.at[turn, landing, pl.ds(0, kinds)]
        elif at == 1:
            source = pack_y.at[turn, side, pl.ds(0, kinds)]
            target = halo_y.at[turn, landing, pl.ds(0, kinds)]
        else:
            source = pack_z.at[turn, side]
            target = halo_z.at[turn, landing]
        return pltpu.make_async_remote_copy(
            src_ref=source,
            dst_ref=target,
            send_sem=send_t.at[turn, at * 2 + side],
            recv_sem=recv_t.at[turn, at * 2 + landing],
            device_id=device,
            device_id_type=MESH,
        )

    def start_faces(slot, turn):
        pack(slot, turn)
        for at, axis in enumerate(AXES):
            for side, (there, device) in enumerate(sides_of(axis)):

                @pl.when(there)
                def _(at=at, side=side, device=device):
                    face_copy(slot, turn, at, side, device, 1 - side).start()

    def wait_faces(slot, turn):
        for at, axis in enumerate(AXES):
            for side, (there, device) in enumerate(sides_of(axis)):

                @pl.when(there)
                def _(at=at, side=side, device=device):
                    face_copy(slot, turn, at, side, device, 1 - side).wait_send()
                    face_copy(slot, turn, at, side, device, side).wait_recv()

    barrier = pltpu.get_barrier_semaphore()
    expected = 0
    for axis in AXES:
        for there, device in sides_of(axis):

            @pl.when(there)
            def _(device=device):
                pl.semaphore_signal(barrier, inc=1, device_id=device, device_id_type=MESH)

            expected = expected + there.astype(jnp.int32)
    pl.semaphore_wait(barrier, expected)

    bounds = [planes * part // CHUNKS for part in range(CHUNKS + 1)]
    neighbours = sides_of("gx")

    def slab_copy(owner, way, hop, part, device):
        view = gathered.at[owner, pl.ds(bounds[part], bounds[part + 1] - bounds[part])]
        return pltpu.make_async_remote_copy(
            src_ref=view,
            dst_ref=view,
            send_sem=send_g.at[way, hop, part],
            recv_sem=recv_g.at[way, hop, part],
            device_id=device,
            device_id_type=MESH,
        )

    def slab_of(way, hop):
        owner = here - hop if way == 1 else here + hop
        valid = owner >= 0 if way == 1 else owner < count
        return lax.clamp(0, owner, count - 1), valid

    for hop in range(count):
        for part in range(CHUNKS):
            for way in range(2):
                owner, valid = slab_of(way, hop)
                there, device = neighbours[way]
                back_device = neighbours[1 - way][1]
                if hop > 0:

                    @pl.when(valid)
                    def _(owner=owner, way=way, hop=hop, part=part, device=back_device):
                        slab_copy(owner, way, hop - 1, part, device).wait_recv()

                if hop < count - 1:

                    @pl.when(jnp.logical_and(valid, there))
                    def _(owner=owner, way=way, hop=hop, part=part, device=device):
                        slab_copy(owner, way, hop, part, device).start()

        if hop == 0:
            start_faces(0, 0)

    for hop in range(count - 1):
        for part in range(CHUNKS):
            for way in range(2):
                owner, valid = slab_of(way, hop)
                there, device = neighbours[way]

                @pl.when(jnp.logical_and(valid, there))
                def _(owner=owner, way=way, hop=hop, part=part, device=device):
                    slab_copy(owner, way, hop, part, device).wait_send()

    indices = swap_indices()
    low = lane < 64

    def arrange(plane, carry):
        for tile in range(4):
            cut = pl.ds(tile * 128, 128)
            first = jnp.concatenate([gathered[0, plane, :, cut], gathered[1, plane, :, cut]], axis=0)
            second = jnp.concatenate([gathered[2, plane, :, cut], gathered[3, plane, :, cut]], axis=0)
            even = jnp.where(low, first, pltpu.roll(second, 64, 1))
            odd = jnp.where(low, pltpu.roll(first, 64, 1), second)
            fields[plane, 2 * tile] = swap(even, indices)
            fields[plane, 2 * tile + 1] = swap(odd, indices)
        return carry

    lax.fori_loop(0, 22, arrange, 0)

    ids = jnp.concatenate([gathered[dev, 22, :, 0:128] for dev in range(4)], axis=0)
    ids = jnp.concatenate([ids, jnp.zeros((112, 128), jnp.float32)], axis=0)
    spread = lax.broadcasted_iota(jnp.int32, (128, 128), 1) // 8
    spread = (spread == lax.broadcasted_iota(jnp.int32, (128, 128), 0)).astype(jnp.float32)
    by_dir = lax.dot_general(
        ids, spread, (((0,), (0,)), ((), ())), preferred_element_type=jnp.float32
    )

    def beside_of(vec):
        at = LATTICE_DIRS.index(vec) - 1
        return jnp.broadcast_to(by_dir[at : at + 1], (8, 128)).astype(jnp.int32)

    has = {(0, 0, 0): jnp.ones((8, 128), jnp.int32)}
    for at, (face_x, face_y, step) in enumerate(TABLE_KEYS):
        inner = block_lane if face_x == 0 and face_y == 0 else beside_of((face_x, face_y, 0))
        cell = cell_lane
        if step:
            crossing = cell_lane == (0 if step > 0 else 7)
            inner = jnp.where(crossing, beside_of((face_x, face_y, -step)), inner)
            cell = (cell_lane - step + 8) % 8
        tables[at] = jnp.clip(inner, 0, 15) * 8 + cell
        has[face_x, face_y, step] = jnp.where(inner >= 0, 1, 0)

    def row_face(vec):
        return row == (0 if vec[1] > 0 else 7)

    for a in range(8):
        bits = fields[20, a].astype(jnp.int32)
        allowed = jnp.zeros((8, 128), jnp.int32)
        for member in range(1, 19):
            vec = LATTICE_DIRS[member]
            face_x = -vec[0] if not 0 <= a - vec[0] <= 7 else 0
            usable = has[face_x, 0, vec[2]]
            if vec[1]:
                usable = jnp.where(row_face(vec), has[face_x, -vec[1], vec[2]], usable)
            allowed = allowed + usable * (1 << (member - 1))
        open_bits[a] = bits & allowed
        flagged = fields[21, a]
        relax = 1.0 / (3.0 * fields[19, a] + 0.5)
        inside = flagged < 0.5
        relax_by[0, a] = jnp.where(inside, relax, 1.0)
        relax_by[1, a] = jnp.where(inside, 0.0, 1.0)
        marks[a] = jnp.where(
            inside, 0.0, jnp.where(flagged < 1.5, INLET_DENSITY, OUTLET_DENSITY)
        )

    def first_collision(a, carry):
        popul = [fields[member, a] * weight_of(member) for member in range(19)]
        density, momentum = moments(popul)
        relax = 1.0 / (3.0 * fields[19, a] + 0.5)
        for member, value in enumerate(relaxed(popul, density, momentum, relax)):
            post[0, member, a] = value
        return carry

    lax.fori_loop(0, 8, first_collision, 0)

    def flow_step(turn, carry):
        now = lax.rem(turn, 2)
        later = 1 - now
        final = jnp.where(turn == FLOW_STEPS - 1, 1, 0)
        for a in range(8):
            bits = open_bits[a]
            popul = [post[now, 0, a]]
            for member in range(1, 19):
                vec = LATTICE_DIRS[member]
                opposite = member + 1 if member % 2 else member - 1
                from_a = a - vec[0]
                face_x = 0 if 0 <= from_a <= 7 else -vec[0]
                source = post[now, member, from_a % 8]
                if vec[1]:
                    source = pltpu.roll(source, vec[1] % 8, 0)
                pulled = source
                key = (face_x, 0, vec[2])
                if key != (0, 0, 0):
                    pulled = take(source, tables[TABLE_KEYS.index(key)], 1)
                if vec[1]:
                    key = (face_x, -vec[1], vec[2])
                    other = take(source, tables[TABLE_KEYS.index(key)], 1)
                    pulled = jnp.where(row_face(vec), other, pulled)
                closed = (bits & (1 << (member - 1))) == 0
                popul.append(jnp.where(closed, post[now, opposite, a], pulled))
            density, momentum = moments(popul)
            mark = marks[a]
            density = jnp.where(mark > 0.0, mark, density)
            for member, value in enumerate(relaxed(popul, density, momentum, relax_by[final, a])):
                post[later, member, a] = value
        return carry

    lax.fori_loop(0, FLOW_STEPS, flow_step, 0)
    last = FLOW_STEPS % 2

    source_lane = jnp.full((8, 128), -1, jnp.int32)
    for block in range(16):
        owner_here = jnp.broadcast_to(owners[:, block : block + 1], (8, 128))
        slot_here = jnp.broadcast_to(slots[:, block : block + 1], (8, 128))
        hit = (owner_here == here) & (slot_here == block_lane)
        source_lane = jnp.where(hit, block * 8 + cell_lane, source_lane)
    filled = source_lane >= 0
    source_lane = jnp.maximum(source_lane, 0)
    for a in range(8):
        _, momentum = moments([post[last, member, a] for member in range(19)])
        for axis in range(3):
            speed = ADVECT_GAIN * jnp.where(filled, take(momentum[axis], source_lane, 1), 0.0)
            winds[2 * axis, a] = jnp.maximum(speed, 0.0)
            winds[2 * axis + 1, a] = -jnp.minimum(speed, 0.0)

    def beside_cells(slot, turn, kind, a):
        center = cells[slot, kind, a]
        result = []
        result.append(halo_x[turn, 0, kind] if a == 0 else cells[slot, kind, a - 1])
        result.append(halo_x[turn, 1, kind] if a == 7 else cells[slot, kind, a + 1])
        for side, spot in ((0, 0), (1, 7)):
            edge = jnp.broadcast_to(halo_y[turn, side, kind, a : a + 1], (8, 128))
            result.append(jnp.where(row == spot, edge, pltpu.roll(center, 1 if side == 0 else 7, 0)))
        for side, spot in ((0, 0), (1, 127)):
            col = kind * 8 + a
            edge = jnp.broadcast_to(halo_z[turn, side, :, col : col + 1], (8, 128))
            result.append(jnp.where(lane == spot, edge, pltpu.roll(center, 1 if side == 0 else 127, 1)))
        return center, result

    def tissue(slot, turn):
        for a in range(8):
            if turn == 0:
                center, around = beside_cells(0, 0, species, a)
                for way in range(6):
                    rates[way, a] = 0.5 * (center + around[way])
            rate = [rates[way, a] for way in range(6)]
            wind = [winds[way, a] for way in range(6)]
            appetite = uptake[a]
            eaten = None
            for kind in range(species):
                center, around = beside_cells(slot, turn, kind, a)
                total = center
                for way in range(6):
                    gain = DIFFUSION_GAIN[kind] * rate[way] + wind[way]
                    total = total + gain * (around[way] - center)
                if kind != 2:
                    eaten_here = appetite * center / (HALF_SATURATION[kind] + jnp.abs(center))
                    total = total - eaten_here
                    if kind == 1:
                        eaten = eaten_here
                else:
                    total = total + 2.0 * eaten
                if turn == TISSUE_STEPS - 1:
                    conc_out[kind, a] = total
                else:
                    cells[1 - slot, kind, a] = total

    upper = here * block_count >= 8
    shift_rows = lax.rem(here * block_count, 8) > 0

    def hand_out(member, carry):
        scale = jnp.where(member == 0, 3.0, jnp.where(member < 7, 18.0, 36.0))
        for tile in range(4):
            even = post[last, member, 2 * tile]
            odd = post[last, member, 2 * tile + 1]
            lower_part = jnp.where(low, even, pltpu.roll(odd, 64, 1))
            upper_part = jnp.where(low, pltpu.roll(even, 64, 1), odd)
            rows = swap(jnp.where(upper, upper_part, lower_part), indices) * scale
            rows = jnp.where(shift_rows, pltpu.roll(rows, 4, 0), rows)
            weighted[member, :, pl.ds(tile * 128, 128)] = rows[0:4]
        return carry

    for turn in range(TISSUE_STEPS):
        slot = turn % 2
        if turn > 0:
            start_faces(slot, turn)
            middle = 19 * turn // (TISSUE_STEPS - 1)
            lax.fori_loop(19 * (turn - 1) // (TISSUE_STEPS - 1), middle, hand_out, 0)
        wait_faces(slot, turn)
        tissue(slot, turn)


def fused(
    populations, viscosity, links, flags, neighbours, owners, slots,
    concentrations, diffusivity, uptake_rate,
):
    count = lax.axis_size("gx")
    block_count = populations.shape[2]
    species = concentrations.shape[0]
    vmem = pl.BlockSpec(memory_space=pltpu.VMEM)
    f32 = jnp.float32
    weighted, conc = pl.pallas_call(
        kernel,
        out_shape=(
            jax.ShapeDtypeStruct((19, block_count, 512), f32),
            jax.ShapeDtypeStruct(concentrations.shape, f32),
        ),
        in_specs=[vmem] * 10,
        out_specs=(vmem, vmem),
        scratch_shapes=[
            pltpu.VMEM((count, 23, block_count, 512), f32),
            pltpu.VMEM((22, 8, 8, 128), f32),
            pltpu.VMEM((2, 19, 8, 8, 128), f32),
            pltpu.VMEM((len(TABLE_KEYS), 8, 128), jnp.int32),
            pltpu.VMEM((8, 8, 128), jnp.int32),
            pltpu.VMEM((2, 8, 8, 128), f32),
            pltpu.VMEM((8, 8, 128), f32),
            pltpu.VMEM((2, species + 1, 8, 8, 128), f32),
            pltpu.VMEM((6, 8, 8, 128), f32),
            pltpu.VMEM((6, 8, 8, 128), f32),
            pltpu.VMEM((TISSUE_STEPS, 2, species + 1, 8, 128), f32),
            pltpu.VMEM((TISSUE_STEPS, 2, species + 1, 8, 128), f32),
            pltpu.VMEM((TISSUE_STEPS, 2, 8, 128), f32),
            pltpu.VMEM((TISSUE_STEPS, 2, species + 1, 8, 128), f32),
            pltpu.VMEM((TISSUE_STEPS, 2, 8, 128), f32),
            pltpu.SemaphoreType.DMA((2, count - 1, CHUNKS)),
            pltpu.SemaphoreType.DMA((2, count - 1, CHUNKS)),
            pltpu.SemaphoreType.DMA((TISSUE_STEPS, 6)),
            pltpu.SemaphoreType.DMA((TISSUE_STEPS, 6)),
        ],
        compiler_params=pltpu.CompilerParams(
            collective_id=0, has_side_effects=True, vmem_limit_bytes=32 * 1024 * 1024
        ),
    )(
        populations[:, 0], viscosity[0], links[0], flags[0], neighbours[0], owners, slots,
        concentrations, diffusivity, uptake_rate,
    )
    return weighted[:, None], conc


def per_device(*arrays):
    populations, concentrations = arrays[0], arrays[7]
    fits = (
        lax.axis_size("gx") == 4
        and populations.shape[2] == 4
        and concentrations.shape[1:] == (8, 8, 128)
    )
    return fused(*arrays) if fits else shards(*arrays)


def solution(mesh):
    return jax.shard_map(
        per_device,
        mesh=mesh,
        in_specs=(
            P(None, ("gy", "gz"), "gx", None),
            P(("gy", "gz"), "gx", None),
            P(("gy", "gz"), "gx", None),
            P(("gy", "gz"), "gx", None),
            P(("gy", "gz"), "gx", None),
            P(("gy", "gz"), None),
            P(("gy", "gz"), None),
            P(None, "gx", "gy", "gz"),
            P("gx", "gy", "gz"),
            P("gx", "gy", "gz"),
        ),
        out_specs=(P(None, ("gy", "gz"), "gx", None), P(None, "gx", "gy", "gz")),
        check_vma=False,
    )
```

```python
import jax
import jax.numpy as jnp
import numpy as np
from jax import lax
from jax.experimental import pallas as pl
from jax.experimental.pallas import tpu as pltpu
from jax.sharding import PartitionSpec as P

FLOW_STEPS = 4
TISSUE_STEPS = 3


LATTICE_DIRS = (
    (0, 0, 0),
    (1, 0, 0),
    (-1, 0, 0),
    (0, 1, 0),
    (0, -1, 0),
    (0, 0, 1),
    (0, 0, -1),
    (1, 1, 0),
    (-1, -1, 0),
    (1, -1, 0),
    (-1, 1, 0),
    (1, 0, 1),
    (-1, 0, -1),
    (1, 0, -1),
    (-1, 0, 1),
    (0, 1, 1),
    (0, -1, -1),
    (0, 1, -1),
    (0, -1, 1),
)
DIFFUSION_GAIN = (1.0, 0.6, 0.7, 0.35)
HALF_SATURATION = (0.3, 0.5, 0.8, 0.2)
ADVECT_GAIN = 3.0
INLET_DENSITY = 1.03
OUTLET_DENSITY = 0.97


def padded(cells, sides, width):
    for axis, dim in sides:
        count = lax.axis_size(axis)
        ends = count - 1
        head = lax.slice_in_dim(cells, 0, width, axis=dim)
        tail = lax.slice_in_dim(cells, cells.shape[dim] - width, cells.shape[dim], axis=dim)
        cells = jnp.concatenate(
            [
                lax.ppermute(tail, axis, [(i, (i + 1) % count) for i in range(ends)]),
                cells,
                lax.ppermute(head, axis, [((i + 1) % count, i) for i in range(ends)]),
            ],
            axis=dim,
        )
    return cells


def lattice_tables():
    vectors = np.array(LATTICE_DIRS, dtype=np.int64)
    weights = np.array([1.0 / 3.0] + [1.0 / 18.0] * 6 + [1.0 / 36.0] * 12)
    opposite = [
        LATTICE_DIRS.index(tuple((-part_val for part_val in LATTICE_DIRS[member])))
        for member in range(19)
    ]
    sites = np.arange(512)
    coords = np.stack([sites // 64, sites // 8 % 8, sites % 8], axis=1)
    stride = np.array([64, 8, 1])
    position = {}
    rim_source = []
    for member in range(1, 19):
        moved = coords + vectors[member]
        leaving = ((moved < 0) | (moved > 7)).any(axis=1)
        chosen = sites[leaving]
        for site_id in chosen:
            position[member, int(site_id)] = len(rim_source)
            rim_source.append(member * 512 + int(site_id))
    rim_width = -(-len(rim_source) // 128) * 128
    request_dir = []
    request_pos = []
    offsets = [0]
    counts = [0]
    selects = [sites.copy()]
    dir_maps = [np.zeros(512, np.int64)]
    arriving_masks = [np.zeros(512, bool)]
    shifts = [0]
    for member in range(1, 19):
        source = coords - vectors[member]
        arriving = ((source < 0) | (source > 7)).any(axis=1)
        select = sites.copy()
        dir_map = np.zeros(512, np.int64)
        offsets.append(len(request_dir))
        counts.append(int(arriving.sum()))
        for rank_pos, site_id in enumerate(sites[arriving]):
            block_dir = tuple((int(part_val) for part_val in source[site_id] // 8))
            dir_index = LATTICE_DIRS.index(block_dir) - 1
            local_site = int((source[site_id] % 8 * stride).sum())
            request_dir.append(dir_index)
            request_pos.append(position[member, local_site])
            select[site_id] = 512 + rank_pos
            dir_map[site_id] = dir_index
        selects.append(select)
        dir_maps.append(dir_map)
        arriving_masks.append(arriving)
        shifts.append(int((vectors[member] * stride).sum()))
    request_width = -(-len(request_dir) // 128) * 128
    request_dir = request_dir + [0] * (request_width - len(request_dir))
    request_pos = request_pos + [0] * (request_width - len(request_pos))
    return {
        "vectors": vectors,
        "weights": weights,
        "opposite": opposite,
        "rim_source": np.array(rim_source),
        "rim_width": rim_width,
        "request_dir": np.array(request_dir),
        "request_pos": np.array(request_pos),
        "offsets": offsets,
        "counts": counts,
        "selects": selects,
        "dir_maps": dir_maps,
        "arriving": arriving_masks,
        "shifts": shifts,
    }


def equilibrium(density, momentum, vectors, weights):
    project = jnp.tensordot(vectors, momentum, axes=1, precision=lax.Precision.HIGHEST)
    square = jnp.sum(momentum * momentum, axis=0)
    return weights[:, None, None] * (
        density + 3.0 * project + 4.5 * project * project - 1.5 * square
    )


def collide(popul, relax, vectors, weights):
    density = jnp.sum(popul, axis=0)
    momentum = jnp.tensordot(vectors.T, popul, axes=1, precision=lax.Precision.HIGHEST)
    return popul - relax * (popul - equilibrium(density, momentum, vectors, weights))


def rim_rows(post, tables):
    block_count = post.shape[1]
    flat = jnp.transpose(post, (1, 0, 2)).reshape(block_count, 19 * 512)
    rim = jnp.take(flat, jnp.asarray(tables["rim_source"], jnp.int32), axis=1)
    return jnp.pad(rim, ((0, 0), (0, tables["rim_width"] - rim.shape[1])))


def stream(post, arrived, link_bits, beside_ids, tables):
    result = [post[0]]
    for member in range(1, 19):
        rolled = jnp.roll(post[member], tables["shifts"][member], axis=-1)
        start_col = tables["offsets"][member]
        pool = jnp.concatenate(
            [rolled, arrived[:, start_col : start_col + tables["counts"][member]]], axis=1
        )
        pulled = jnp.take(pool, jnp.asarray(tables["selects"][member], jnp.int32), axis=1)
        beside = (
            jnp.take(beside_ids, jnp.asarray(tables["dir_maps"][member], jnp.int32), axis=1) >= 0
        )
        link_open = jnp.right_shift(link_bits, member - 1) % 2 == 1
        arriving = jnp.asarray(tables["arriving"][member])[None, :]
        opened = link_open & (beside | jnp.logical_not(arriving))
        result.append(jnp.where(opened, pulled, post[tables["opposite"][member]]))
    return jnp.stack(result)


def boundary(popul, site_flags, vectors, weights):
    momentum = jnp.tensordot(vectors.T, popul, axes=1, precision=lax.Precision.HIGHEST)
    density = jnp.where(site_flags == 1, INLET_DENSITY, OUTLET_DENSITY)
    settled = equilibrium(density, momentum, vectors, weights)
    return jnp.where(site_flags[None] > 0, settled, popul)


def shifted(field, offset):
    extent_x, extent_y, extent_z = field.shape[-3:]
    step_x, step_y, step_z = offset
    return field[
        ...,
        1 + step_x : extent_x - 1 + step_x,
        1 + step_y : extent_y - 1 + step_y,
        1 + step_z : extent_z - 1 + step_z,
    ]


def tissue_step(conc_ext, diff_ext, uptake_here, velocity):
    center = conc_ext[:, 1:-1, 1:-1, 1:-1]
    diff_mid = diff_ext[1:-1, 1:-1, 1:-1]
    spread = jnp.zeros_like(center)
    for offset in ((1, 0, 0), (-1, 0, 0), (0, 1, 0), (0, -1, 0), (0, 0, 1), (0, 0, -1)):
        beside_conc = shifted(conc_ext, offset)
        beside_diff = shifted(diff_ext, offset)
        spread = spread + 0.5 * (diff_mid + beside_diff) * (beside_conc - center)
    drifted = jnp.zeros_like(center)
    for axis_pos in range(3):
        unit_vec = [0, 0, 0]
        unit_vec[axis_pos] = 1
        ahead = shifted(conc_ext, tuple(unit_vec))
        behind = shifted(conc_ext, tuple((-part_val for part_val in unit_vec)))
        speed_axis = ADVECT_GAIN * velocity[axis_pos]
        drifted = (
            drifted
            - jnp.maximum(speed_axis, 0.0) * (center - behind)
            - jnp.minimum(speed_axis, 0.0) * (ahead - center)
        )
    species_gain = jnp.array(DIFFUSION_GAIN, jnp.float32)[:, None, None, None]
    halfsat = jnp.array(HALF_SATURATION, jnp.float32)[:, None, None, None]
    uptake = uptake_here * center / (halfsat + jnp.abs(center))
    reaction = jnp.stack([-uptake[0], -uptake[1], 2.0 * uptake[1], -uptake[3]])
    return center + species_gain * spread + drifted + reaction


def shards(
    populations,
    viscosity,
    links,
    flags,
    neighbours,
    owners,
    slots,
    concentrations,
    diffusivity,
    uptake_rate,
):
    tables = lattice_tables()
    weights = jnp.asarray(tables["weights"], jnp.float32)
    vectors = jnp.asarray(tables["vectors"], jnp.float32)
    popul = populations[:, 0] * weights[:, None, None]
    relax = 1.0 / (3.0 * viscosity[0] + 0.5)
    link_bits = links[0]
    site_flags = flags[0]
    beside_ids = neighbours[0]
    block_count = popul.shape[1]
    request_block = jnp.take(beside_ids, jnp.asarray(tables["request_dir"], jnp.int32), axis=1)
    request_pos = jnp.asarray(tables["request_pos"], jnp.int32)
    first_block = (lax.axis_index("gx") - 1) * block_count
    local_block = request_block - first_block
    valid = (local_block >= 0) & (local_block < 3 * block_count)
    for turn_index in range(FLOW_STEPS):
        post = collide(popul, relax, vectors, weights)
        rim = rim_rows(post, tables)
        extended = padded(rim, (("gx", 0),), block_count)
        flat_index = (
            jnp.clip(local_block, 0, 3 * block_count - 1) * extended.shape[1] + request_pos[None, :]
        )
        arrived = jnp.where(valid, jnp.take(extended.reshape(-1), flat_index), 0.0)
        popul = stream(post, arrived, link_bits, beside_ids, tables)
        popul = boundary(popul, site_flags, vectors, weights)
    weighted = (popul / weights[:, None, None])[:, None]
    momentum = jnp.tensordot(vectors.T, popul, axes=1, precision=lax.Precision.HIGHEST)
    block_rows = jnp.transpose(momentum, (1, 0, 2)).reshape(block_count, 3 * 512)
    extent_x, extent_y, extent_z = concentrations.shape[1:]
    slot_x = extent_x // 8
    slot_y = extent_y // 8
    slot_z = extent_z // 8
    slot_total = slot_x * slot_y * slot_z
    owner_all = owners[0]
    slot_all = slots[0]
    my_index = lax.axis_index("gx")
    slot_ids = jnp.arange(slot_total, dtype=jnp.int32)
    start_blocks = jnp.zeros((slot_total, 3 * 512), jnp.float32)
    piece = jax.tree.map(lambda part: lax.all_gather(part, "gx", axis=0, tiled=True), block_rows)
    row_count = piece.shape[0]
    piece_owner = lax.slice_in_dim(owner_all, 0, row_count, axis=0)
    piece_slot = lax.slice_in_dim(slot_all, 0, row_count, axis=0)
    hit = (piece_owner[None, :] == my_index) & (piece_slot[None, :] == slot_ids[:, None])
    brick_blocks = start_blocks + jnp.dot(
        hit.astype(jnp.float32), piece, precision=lax.Precision.HIGHEST
    )
    velocity = (
        brick_blocks.reshape(slot_x, slot_y, slot_z, 3, 8, 8, 8)
        .transpose(3, 0, 4, 1, 5, 2, 6)
        .reshape(3, extent_x, extent_y, extent_z)
    )
    conc_ext, diff_ext = (
        padded(concentrations, (("gx", 1), ("gy", 2), ("gz", 3)), 1),
        padded(diffusivity[None], (("gx", 1), ("gy", 2), ("gz", 3)), 1),
    )
    diff_ext = diff_ext[0]
    conc = tissue_step(conc_ext, diff_ext, uptake_rate, velocity)
    for turn_index in range(TISSUE_STEPS - 1):
        conc_ext = padded(conc, (("gx", 1), ("gy", 2), ("gz", 3)), 1)
        conc = tissue_step(conc_ext, diff_ext, uptake_rate, velocity)
    return (weighted, conc)


MESH = pl.DeviceIdType.MESH
AXES = ("gx", "gy", "gz")
CHUNKS = 2


def iota(axis):
    return lax.broadcasted_iota(jnp.int32, (8, 128), axis)


def take(values, index, axis):
    return jnp.take_along_axis(values, index, axis=axis, mode="promise_in_bounds")


def swap_indices():
    row, lane = iota(0), iota(1)
    half, group, cell = lane // 64, (lane // 8) % 8, lane % 8
    ahead = half * 64 + ((group + row) % 8) * 8 + cell
    rows = (row - group + 8) % 8
    back = half * 64 + rows * 8 + cell
    return ahead, rows, back


def swap(values, indices):
    ahead, rows, back = indices
    return take(take(take(values, ahead, 1), rows, 0), back, 1)


def tables_needed():
    keys = []
    for vec in LATTICE_DIRS[1:]:
        for face_x in {0, -vec[0]}:
            for face_y in {0, -vec[1]}:
                key = (face_x, face_y, vec[2])
                if key != (0, 0, 0) and key not in keys:
                    keys.append(key)
    return sorted(keys)


TABLE_KEYS = tables_needed()


def weight_of(member):
    return 1.0 / 3.0 if member == 0 else (1.0 / 18.0 if member < 7 else 1.0 / 36.0)


def moments(popul):
    density = popul[0]
    momentum = [None, None, None]
    for member in range(1, 19):
        density = density + popul[member]
        for axis in range(3):
            sign = LATTICE_DIRS[member][axis]
            if sign:
                term = popul[member]
                if momentum[axis] is None:
                    momentum[axis] = term if sign > 0 else -term
                else:
                    momentum[axis] = momentum[axis] + term if sign > 0 else momentum[axis] - term
    return density, momentum


def relaxed(popul, density, momentum, relax):
    square = momentum[0] * momentum[0] + momentum[1] * momentum[1] + momentum[2] * momentum[2]
    rest = density - 1.5 * square
    result = [popul[0] - relax * (popul[0] - rest * (1.0 / 3.0))]
    for member in range(1, 19, 2):
        vec = LATTICE_DIRS[member]
        weight = weight_of(member)
        project = None
        for axis in range(3):
            if vec[axis]:
                term = momentum[axis]
                if project is None:
                    project = term if vec[axis] > 0 else -term
                else:
                    project = project + term if vec[axis] > 0 else project - term
        even = weight * rest + (4.5 * weight) * (project * project)
        odd = (3.0 * weight) * project
        result.append(popul[member] - relax * (popul[member] - (even + odd)))
        result.append(popul[member + 1] - relax * (popul[member + 1] - (even - odd)))
    return result


def sides_of(axis):
    count = lax.axis_size(axis)
    here = lax.axis_index(axis)
    return (
        (here > 0, {axis: lax.max(here - 1, 0)}),
        (here < count - 1, {axis: lax.min(here + 1, count - 1)}),
    )


def kernel(
    pops, visc, links, flags, beside, owners_in, slots_in, conc, diff, uptake_in,
    weighted, conc_out,
    links_at, flags_at, beside_at, owners, slots, uptake, gathered, fields, post, tables, open_bits, relax_by, marks,
    cells, rates, winds, halo_x, halo_y, halo_z, pack_y, pack_z,
    load, send_g, recv_g, send_t, recv_t,
):
    count = lax.axis_size("gx")
    here = lax.axis_index("gx")
    block_count = pops.shape[1]
    species = conc.shape[0]
    planes = gathered.shape[1]
    lane, row = iota(1), iota(0)
    block_lane, cell_lane = lane // 8, lane % 8
    halos = (halo_x, halo_y, halo_z)

    pairs = (
        (pops, gathered.at[here, pl.ds(0, 19)]),
        (visc, gathered.at[here, 19]),
        (links, links_at),
        (flags, flags_at),
        (beside, beside_at),
        (conc, cells.at[0, pl.ds(0, species)]),
        (diff, cells.at[0, species]),
        (uptake_in, uptake),
        (owners_in, owners),
        (slots_in, slots),
    )
    loads = [pltpu.make_async_copy(src, dst, load.at[at]) for at, (src, dst) in enumerate(pairs)]
    for copy in loads:
        copy.start()

    for at, axis in enumerate(AXES):
        for side, (there, _) in enumerate(sides_of(axis)):

            @pl.when(jnp.logical_not(there))
            def _(at=at, side=side):
                for turn in range(TISSUE_STEPS):
                    halos[at][turn, side] = jnp.zeros(halos[at].shape[2:], jnp.float32)

    def pack(slot, turn):
        kinds = species + 1 if turn == 0 else species
        for side, spot in ((0, 0), (1, 7)):
            zcol = 0 if side == 0 else 127
            packed = jnp.zeros((8, 128), jnp.float32)
            for kind in range(kinds):
                for a in range(8):
                    tile = cells[slot, kind, a]
                    pack_y[turn, side, kind, a : a + 1] = tile[spot : spot + 1]
                    packed = jnp.where(
                        lane == kind * 8 + a,
                        jnp.broadcast_to(tile[:, zcol : zcol + 1], (8, 128)),
                        packed,
                    )
            pack_z[turn, side] = packed

    def face_copy(slot, turn, at, side, device, landing):
        kinds = species + 1 if turn == 0 else species
        if at == 0:
            source = cells.at[slot, pl.ds(0, kinds), 0 if side == 0 else 7]
            target = halo_x.at[turn, landing, pl.ds(0, kinds)]
        elif at == 1:
            source = pack_y.at[turn, side, pl.ds(0, kinds)]
            target = halo_y.at[turn, landing, pl.ds(0, kinds)]
        else:
            source = pack_z.at[turn, side]
            target = halo_z.at[turn, landing]
        return pltpu.make_async_remote_copy(
            src_ref=source,
            dst_ref=target,
            send_sem=send_t.at[turn, at * 2 + side],
            recv_sem=recv_t.at[turn, at * 2 + landing],
            device_id=device,
            device_id_type=MESH,
        )

    def start_faces(slot, turn):
        pack(slot, turn)
        for at, axis in enumerate(AXES):
            for side, (there, device) in enumerate(sides_of(axis)):

                @pl.when(there)
                def _(at=at, side=side, device=device):
                    face_copy(slot, turn, at, side, device, 1 - side).start()

    def wait_faces(slot, turn):
        for at, axis in enumerate(AXES):
            for side, (there, device) in enumerate(sides_of(axis)):

                @pl.when(there)
                def _(at=at, side=side, device=device):
                    face_copy(slot, turn, at, side, device, 1 - side).wait_send()
                    face_copy(slot, turn, at, side, device, side).wait_recv()

    barrier = pltpu.get_barrier_semaphore()
    expected = 0
    for axis in AXES:
        for there, device in sides_of(axis):

            @pl.when(there)
            def _(device=device):
                pl.semaphore_signal(barrier, inc=1, device_id=device, device_id_type=MESH)

            expected = expected + there.astype(jnp.int32)
    for copy in loads[:5]:
        copy.wait()
    gathered[here, 20] = links_at[...].astype(jnp.float32)
    gathered[here, 21] = flags_at[...].astype(jnp.float32)
    gathered[here, 22] = jnp.zeros((block_count, 512), jnp.float32)
    gathered[here, 22, :, 0:18] = beside_at[...].astype(jnp.float32)
    pl.semaphore_wait(barrier, expected)

    bounds = [planes * part // CHUNKS for part in range(CHUNKS + 1)]
    neighbours = sides_of("gx")

    def slab_copy(owner, way, hop, part, device):
        view = gathered.at[owner, pl.ds(bounds[part], bounds[part + 1] - bounds[part])]
        return pltpu.make_async_remote_copy(
            src_ref=view,
            dst_ref=view,
            send_sem=send_g.at[way, hop, part],
            recv_sem=recv_g.at[way, hop, part],
            device_id=device,
            device_id_type=MESH,
        )

    def slab_of(way, hop):
        owner = here - hop if way == 1 else here + hop
        valid = owner >= 0 if way == 1 else owner < count
        return lax.clamp(0, owner, count - 1), valid

    indices = swap_indices()
    ahead, rows, _ = indices
    spots = [
        [half * 64 + ((row - 4 * late - block_lane % block_count + 16) % 8) * 8 + cell_lane
         for half in range(2)]
        for late in range(2)
    ]

    def absorb(owner, first):
        mine = lane // (8 * block_count) == owner

        def one(plane):
            for pair in range(2):
                both = jnp.concatenate(
                    [gathered[owner, plane, :, pl.ds((2 * pair + late) * 128, 128)]
                     for late in range(2)],
                    axis=0,
                )
                both = take(take(both, ahead, 1), rows, 0)
                for late in range(2):
                    for half in range(2):
                        a = 2 * (2 * pair + late) + half
                        moved = take(both, spots[late][half], 1)
                        if not first:
                            moved = jnp.where(mine, moved, fields[plane, a])
                        fields[plane, a] = moved

        def two(at, carry):
            one(2 * at)
            one(2 * at + 1)
            return carry

        lax.fori_loop(0, 11, two, 0)

    for hop in range(count):
        for part in range(CHUNKS):
            for way in range(2):
                owner, valid = slab_of(way, hop)
                there, device = neighbours[way]
                back_device = neighbours[1 - way][1]
                if hop > 0:

                    @pl.when(valid)
                    def _(owner=owner, way=way, hop=hop, part=part, device=back_device):
                        slab_copy(owner, way, hop - 1, part, device).wait_recv()

                if hop < count - 1:

                    @pl.when(jnp.logical_and(valid, there))
                    def _(owner=owner, way=way, hop=hop, part=part, device=device):
                        slab_copy(owner, way, hop, part, device).start()

        if hop == 0:
            for copy in loads[5:]:
                copy.wait()
            start_faces(0, 0)
            absorb(here, True)
        else:
            for way in range(2):
                owner, valid = slab_of(way, hop)

                @pl.when(valid)
                def _(owner=owner):
                    absorb(owner, False)

    for hop in range(count - 1):
        for part in range(CHUNKS):
            for way in range(2):
                owner, valid = slab_of(way, hop)
                there, device = neighbours[way]

                @pl.when(jnp.logical_and(valid, there))
                def _(owner=owner, way=way, hop=hop, part=part, device=device):
                    slab_copy(owner, way, hop, part, device).wait_send()

    low = lane < 64
    ids = jnp.concatenate([gathered[dev, 22, :, 0:128] for dev in range(4)], axis=0)
    ids = jnp.concatenate([ids, jnp.zeros((112, 128), jnp.float32)], axis=0)
    spread = lax.broadcasted_iota(jnp.int32, (128, 128), 1) // 8
    spread = (spread == lax.broadcasted_iota(jnp.int32, (128, 128), 0)).astype(jnp.float32)
    by_dir = lax.dot_general(
        ids, spread, (((0,), (0,)), ((), ())), preferred_element_type=jnp.float32
    )

    def beside_of(vec):
        at = LATTICE_DIRS.index(vec) - 1
        return jnp.broadcast_to(by_dir[at : at + 1], (8, 128)).astype(jnp.int32)

    has = {(0, 0, 0): jnp.ones((8, 128), jnp.int32)}
    for at, (face_x, face_y, step) in enumerate(TABLE_KEYS):
        inner = block_lane if face_x == 0 and face_y == 0 else beside_of((face_x, face_y, 0))
        cell = cell_lane
        if step:
            crossing = cell_lane == (0 if step > 0 else 7)
            inner = jnp.where(crossing, beside_of((face_x, face_y, -step)), inner)
            cell = (cell_lane - step + 8) % 8
        tables[at] = jnp.clip(inner, 0, 15) * 8 + cell
        has[face_x, face_y, step] = jnp.where(inner >= 0, 1, 0)

    def row_face(vec):
        return row == (0 if vec[1] > 0 else 7)

    for a in range(8):
        bits = fields[20, a].astype(jnp.int32)
        allowed = jnp.zeros((8, 128), jnp.int32)
        for member in range(1, 19):
            vec = LATTICE_DIRS[member]
            face_x = -vec[0] if not 0 <= a - vec[0] <= 7 else 0
            usable = has[face_x, 0, vec[2]]
            if vec[1]:
                usable = jnp.where(row_face(vec), has[face_x, -vec[1], vec[2]], usable)
            allowed = allowed + usable * (1 << (member - 1))
        open_bits[a] = bits & allowed
        flagged = fields[21, a]
        relax = 1.0 / (3.0 * fields[19, a] + 0.5)
        inside = flagged < 0.5
        relax_by[0, a] = jnp.where(inside, relax, 1.0)
        relax_by[1, a] = jnp.where(inside, 0.0, 1.0)
        marks[a] = jnp.where(
            inside, 0.0, jnp.where(flagged < 1.5, INLET_DENSITY, OUTLET_DENSITY)
        )

    def first_collision(a, carry):
        popul = [fields[member, a] * weight_of(member) for member in range(19)]
        density, momentum = moments(popul)
        relax = 1.0 / (3.0 * fields[19, a] + 0.5)
        for member, value in enumerate(relaxed(popul, density, momentum, relax)):
            post[0, member, a] = value
        return carry

    lax.fori_loop(0, 8, first_collision, 0)

    def flow_step(turn, carry):
        now = lax.rem(turn, 2)
        later = 1 - now
        final = jnp.where(turn == FLOW_STEPS - 1, 1, 0)
        for a in range(8):
            bits = open_bits[a]
            popul = [post[now, 0, a]]
            for member in range(1, 19):
                vec = LATTICE_DIRS[member]
                opposite = member + 1 if member % 2 else member - 1
                from_a = a - vec[0]
                face_x = 0 if 0 <= from_a <= 7 else -vec[0]
                source = post[now, member, from_a % 8]
                if vec[1]:
                    source = pltpu.roll(source, vec[1] % 8, 0)
                pulled = source
                key = (face_x, 0, vec[2])
                if key != (0, 0, 0):
                    pulled = take(source, tables[TABLE_KEYS.index(key)], 1)
                if vec[1]:
                    key = (face_x, -vec[1], vec[2])
                    other = take(source, tables[TABLE_KEYS.index(key)], 1)
                    pulled = jnp.where(row_face(vec), other, pulled)
                closed = (bits & (1 << (member - 1))) == 0
                popul.append(jnp.where(closed, post[now, opposite, a], pulled))
            density, momentum = moments(popul)
            mark = marks[a]
            density = jnp.where(mark > 0.0, mark, density)
            for member, value in enumerate(relaxed(popul, density, momentum, relax_by[final, a])):
                post[later, member, a] = value
        return carry

    lax.fori_loop(0, FLOW_STEPS, flow_step, 0)
    last = FLOW_STEPS % 2

    source_lane = jnp.full((8, 128), -1, jnp.int32)
    for block in range(16):
        owner_here = jnp.broadcast_to(owners[:, block : block + 1], (8, 128))
        slot_here = jnp.broadcast_to(slots[:, block : block + 1], (8, 128))
        hit = (owner_here == here) & (slot_here == block_lane)
        source_lane = jnp.where(hit, block * 8 + cell_lane, source_lane)
    filled = source_lane >= 0
    source_lane = jnp.maximum(source_lane, 0)
    for a in range(8):
        _, momentum = moments([post[last, member, a] for member in range(19)])
        for axis in range(3):
            speed = ADVECT_GAIN * jnp.where(filled, take(momentum[axis], source_lane, 1), 0.0)
            winds[2 * axis, a] = jnp.maximum(speed, 0.0)
            winds[2 * axis + 1, a] = -jnp.minimum(speed, 0.0)

    def beside_cells(slot, turn, kind, a):
        center = cells[slot, kind, a]
        result = []
        result.append(halo_x[turn, 0, kind] if a == 0 else cells[slot, kind, a - 1])
        result.append(halo_x[turn, 1, kind] if a == 7 else cells[slot, kind, a + 1])
        for side, spot in ((0, 0), (1, 7)):
            edge = jnp.broadcast_to(halo_y[turn, side, kind, a : a + 1], (8, 128))
            result.append(jnp.where(row == spot, edge, pltpu.roll(center, 1 if side == 0 else 7, 0)))
        for side, spot in ((0, 0), (1, 127)):
            col = kind * 8 + a
            edge = jnp.broadcast_to(halo_z[turn, side, :, col : col + 1], (8, 128))
            result.append(jnp.where(lane == spot, edge, pltpu.roll(center, 1 if side == 0 else 127, 1)))
        return center, result

    def tissue(slot, turn):
        for a in range(8):
            if turn == 0:
                center, around = beside_cells(0, 0, species, a)
                for way in range(6):
                    rates[way, a] = 0.5 * (center + around[way])
            rate = [rates[way, a] for way in range(6)]
            wind = [winds[way, a] for way in range(6)]
            appetite = uptake[a]
            eaten = None
            for kind in range(species):
                center, around = beside_cells(slot, turn, kind, a)
                total = center
                for way in range(6):
                    gain = DIFFUSION_GAIN[kind] * rate[way] + wind[way]
                    total = total + gain * (around[way] - center)
                if kind != 2:
                    eaten_here = appetite * center / (HALF_SATURATION[kind] + jnp.abs(center))
                    total = total - eaten_here
                    if kind == 1:
                        eaten = eaten_here
                else:
                    total = total + 2.0 * eaten
                if turn == TISSUE_STEPS - 1:
                    conc_out[kind, a] = total
                else:
                    cells[1 - slot, kind, a] = total

    upper = here * block_count >= 8
    shift_rows = lax.rem(here * block_count, 8) > 0

    def hand_out_one(member):
        scale = jnp.where(jnp.asarray(member) == 0, 3.0, jnp.where(jnp.asarray(member) < 7, 18.0, 36.0))
        for tile in range(4):
            even = post[last, member, 2 * tile]
            odd = post[last, member, 2 * tile + 1]
            lower_part = jnp.where(low, even, pltpu.roll(odd, 64, 1))
            upper_part = jnp.where(low, pltpu.roll(even, 64, 1), odd)
            rows = swap(jnp.where(upper, upper_part, lower_part), indices) * scale
            rows = jnp.where(shift_rows, pltpu.roll(rows, 4, 0), rows)
            weighted[member, :, pl.ds(tile * 128, 128)] = rows[0:4]

    def hand_out(first, end):
        def three(at, carry):
            for more in range(3):
                hand_out_one(first + 3 * at + more)
            return carry

        lax.fori_loop(0, (end - first) // 3, three, 0)
        for member in range(end - (end - first) % 3, end):
            hand_out_one(member)

    for turn in range(TISSUE_STEPS):
        slot = turn % 2
        if turn > 0:
            start_faces(slot, turn)
            first = 19 * (turn - 1) // (TISSUE_STEPS - 1)
            hand_out(first, 19 * turn // (TISSUE_STEPS - 1))
        wait_faces(slot, turn)
        tissue(slot, turn)


def fused(
    populations, viscosity, links, flags, neighbours, owners, slots,
    concentrations, diffusivity, uptake_rate,
):
    count = lax.axis_size("gx")
    block_count = populations.shape[2]
    species = concentrations.shape[0]
    vmem = pl.BlockSpec(memory_space=pltpu.VMEM)
    f32 = jnp.float32
    weighted, conc = pl.pallas_call(
        kernel,
        out_shape=(
            jax.ShapeDtypeStruct((19, block_count, 512), f32),
            jax.ShapeDtypeStruct(concentrations.shape, f32),
        ),
        in_specs=[pl.BlockSpec(memory_space=pltpu.HBM)] * 10,
        out_specs=(vmem, vmem),
        scratch_shapes=[
            pltpu.VMEM((block_count, 512), jnp.int32),
            pltpu.VMEM((block_count, 512), jnp.int32),
            pltpu.VMEM((block_count, 18), jnp.int32),
            pltpu.VMEM(owners.shape, jnp.int32),
            pltpu.VMEM(slots.shape, jnp.int32),
            pltpu.VMEM(uptake_rate.shape, f32),
            pltpu.VMEM((count, 23, block_count, 512), f32),
            pltpu.VMEM((22, 8, 8, 128), f32),
            pltpu.VMEM((2, 19, 8, 8, 128), f32),
            pltpu.VMEM((len(TABLE_KEYS), 8, 128), jnp.int32),
            pltpu.VMEM((8, 8, 128), jnp.int32),
            pltpu.VMEM((2, 8, 8, 128), f32),
            pltpu.VMEM((8, 8, 128), f32),
            pltpu.VMEM((2, species + 1, 8, 8, 128), f32),
            pltpu.VMEM((6, 8, 8, 128), f32),
            pltpu.VMEM((6, 8, 8, 128), f32),
            pltpu.VMEM((TISSUE_STEPS, 2, species + 1, 8, 128), f32),
            pltpu.VMEM((TISSUE_STEPS, 2, species + 1, 8, 128), f32),
            pltpu.VMEM((TISSUE_STEPS, 2, 8, 128), f32),
            pltpu.VMEM((TISSUE_STEPS, 2, species + 1, 8, 128), f32),
            pltpu.VMEM((TISSUE_STEPS, 2, 8, 128), f32),
            pltpu.SemaphoreType.DMA((10,)),
            pltpu.SemaphoreType.DMA((2, count - 1, CHUNKS)),
            pltpu.SemaphoreType.DMA((2, count - 1, CHUNKS)),
            pltpu.SemaphoreType.DMA((TISSUE_STEPS, 6)),
            pltpu.SemaphoreType.DMA((TISSUE_STEPS, 6)),
        ],
        compiler_params=pltpu.CompilerParams(
            collective_id=0, has_side_effects=True, vmem_limit_bytes=64 * 1024 * 1024
        ),
    )(
        populations[:, 0], viscosity[0], links[0], flags[0], neighbours[0], owners, slots,
        concentrations, diffusivity, uptake_rate,
    )
    return weighted[:, None], conc


def per_device(*arrays):
    populations, concentrations = arrays[0], arrays[7]
    fits = (
        lax.axis_size("gx") == 4
        and populations.shape[2] == 4
        and concentrations.shape[1:] == (8, 8, 128)
    )
    return fused(*arrays) if fits else shards(*arrays)


def solution(mesh):
    return jax.shard_map(
        per_device,
        mesh=mesh,
        in_specs=(
            P(None, ("gy", "gz"), "gx", None),
            P(("gy", "gz"), "gx", None),
            P(("gy", "gz"), "gx", None),
            P(("gy", "gz"), "gx", None),
            P(("gy", "gz"), "gx", None),
            P(("gy", "gz"), None),
            P(("gy", "gz"), None),
            P(None, "gx", "gy", "gz"),
            P("gx", "gy", "gz"),
            P("gx", "gy", "gz"),
        ),
        out_specs=(P(None, ("gy", "gz"), "gx", None), P(None, "gx", "gy", "gz")),
        check_vma=False,
    )
```

```python
import jax
import jax.numpy as jnp
import numpy as np
from jax import lax
from jax.experimental import pallas as pl
from jax.experimental.pallas import tpu as pltpu
from jax.sharding import PartitionSpec as P

FLOW_STEPS = 4
TISSUE_STEPS = 3


LATTICE_DIRS = (
    (0, 0, 0),
    (1, 0, 0),
    (-1, 0, 0),
    (0, 1, 0),
    (0, -1, 0),
    (0, 0, 1),
    (0, 0, -1),
    (1, 1, 0),
    (-1, -1, 0),
    (1, -1, 0),
    (-1, 1, 0),
    (1, 0, 1),
    (-1, 0, -1),
    (1, 0, -1),
    (-1, 0, 1),
    (0, 1, 1),
    (0, -1, -1),
    (0, 1, -1),
    (0, -1, 1),
)
DIFFUSION_GAIN = (1.0, 0.6, 0.7, 0.35)
HALF_SATURATION = (0.3, 0.5, 0.8, 0.2)
ADVECT_GAIN = 3.0
INLET_DENSITY = 1.03
OUTLET_DENSITY = 0.97


def padded(cells, sides, width):
    for axis, dim in sides:
        count = lax.axis_size(axis)
        ends = count - 1
        head = lax.slice_in_dim(cells, 0, width, axis=dim)
        tail = lax.slice_in_dim(cells, cells.shape[dim] - width, cells.shape[dim], axis=dim)
        cells = jnp.concatenate(
            [
                lax.ppermute(tail, axis, [(i, (i + 1) % count) for i in range(ends)]),
                cells,
                lax.ppermute(head, axis, [((i + 1) % count, i) for i in range(ends)]),
            ],
            axis=dim,
        )
    return cells


def lattice_tables():
    vectors = np.array(LATTICE_DIRS, dtype=np.int64)
    weights = np.array([1.0 / 3.0] + [1.0 / 18.0] * 6 + [1.0 / 36.0] * 12)
    opposite = [
        LATTICE_DIRS.index(tuple((-part_val for part_val in LATTICE_DIRS[member])))
        for member in range(19)
    ]
    sites = np.arange(512)
    coords = np.stack([sites // 64, sites // 8 % 8, sites % 8], axis=1)
    stride = np.array([64, 8, 1])
    position = {}
    rim_source = []
    for member in range(1, 19):
        moved = coords + vectors[member]
        leaving = ((moved < 0) | (moved > 7)).any(axis=1)
        chosen = sites[leaving]
        for site_id in chosen:
            position[member, int(site_id)] = len(rim_source)
            rim_source.append(member * 512 + int(site_id))
    rim_width = -(-len(rim_source) // 128) * 128
    request_dir = []
    request_pos = []
    offsets = [0]
    counts = [0]
    selects = [sites.copy()]
    dir_maps = [np.zeros(512, np.int64)]
    arriving_masks = [np.zeros(512, bool)]
    shifts = [0]
    for member in range(1, 19):
        source = coords - vectors[member]
        arriving = ((source < 0) | (source > 7)).any(axis=1)
        select = sites.copy()
        dir_map = np.zeros(512, np.int64)
        offsets.append(len(request_dir))
        counts.append(int(arriving.sum()))
        for rank_pos, site_id in enumerate(sites[arriving]):
            block_dir = tuple((int(part_val) for part_val in source[site_id] // 8))
            dir_index = LATTICE_DIRS.index(block_dir) - 1
            local_site = int((source[site_id] % 8 * stride).sum())
            request_dir.append(dir_index)
            request_pos.append(position[member, local_site])
            select[site_id] = 512 + rank_pos
            dir_map[site_id] = dir_index
        selects.append(select)
        dir_maps.append(dir_map)
        arriving_masks.append(arriving)
        shifts.append(int((vectors[member] * stride).sum()))
    request_width = -(-len(request_dir) // 128) * 128
    request_dir = request_dir + [0] * (request_width - len(request_dir))
    request_pos = request_pos + [0] * (request_width - len(request_pos))
    return {
        "vectors": vectors,
        "weights": weights,
        "opposite": opposite,
        "rim_source": np.array(rim_source),
        "rim_width": rim_width,
        "request_dir": np.array(request_dir),
        "request_pos": np.array(request_pos),
        "offsets": offsets,
        "counts": counts,
        "selects": selects,
        "dir_maps": dir_maps,
        "arriving": arriving_masks,
        "shifts": shifts,
    }


def equilibrium(density, momentum, vectors, weights):
    project = jnp.tensordot(vectors, momentum, axes=1, precision=lax.Precision.HIGHEST)
    square = jnp.sum(momentum * momentum, axis=0)
    return weights[:, None, None] * (
        density + 3.0 * project + 4.5 * project * project - 1.5 * square
    )


def collide(popul, relax, vectors, weights):
    density = jnp.sum(popul, axis=0)
    momentum = jnp.tensordot(vectors.T, popul, axes=1, precision=lax.Precision.HIGHEST)
    return popul - relax * (popul - equilibrium(density, momentum, vectors, weights))


def rim_rows(post, tables):
    block_count = post.shape[1]
    flat = jnp.transpose(post, (1, 0, 2)).reshape(block_count, 19 * 512)
    rim = jnp.take(flat, jnp.asarray(tables["rim_source"], jnp.int32), axis=1)
    return jnp.pad(rim, ((0, 0), (0, tables["rim_width"] - rim.shape[1])))


def stream(post, arrived, link_bits, beside_ids, tables):
    result = [post[0]]
    for member in range(1, 19):
        rolled = jnp.roll(post[member], tables["shifts"][member], axis=-1)
        start_col = tables["offsets"][member]
        pool = jnp.concatenate(
            [rolled, arrived[:, start_col : start_col + tables["counts"][member]]], axis=1
        )
        pulled = jnp.take(pool, jnp.asarray(tables["selects"][member], jnp.int32), axis=1)
        beside = (
            jnp.take(beside_ids, jnp.asarray(tables["dir_maps"][member], jnp.int32), axis=1) >= 0
        )
        link_open = jnp.right_shift(link_bits, member - 1) % 2 == 1
        arriving = jnp.asarray(tables["arriving"][member])[None, :]
        opened = link_open & (beside | jnp.logical_not(arriving))
        result.append(jnp.where(opened, pulled, post[tables["opposite"][member]]))
    return jnp.stack(result)


def boundary(popul, site_flags, vectors, weights):
    momentum = jnp.tensordot(vectors.T, popul, axes=1, precision=lax.Precision.HIGHEST)
    density = jnp.where(site_flags == 1, INLET_DENSITY, OUTLET_DENSITY)
    settled = equilibrium(density, momentum, vectors, weights)
    return jnp.where(site_flags[None] > 0, settled, popul)


def shifted(field, offset):
    extent_x, extent_y, extent_z = field.shape[-3:]
    step_x, step_y, step_z = offset
    return field[
        ...,
        1 + step_x : extent_x - 1 + step_x,
        1 + step_y : extent_y - 1 + step_y,
        1 + step_z : extent_z - 1 + step_z,
    ]


def tissue_step(conc_ext, diff_ext, uptake_here, velocity):
    center = conc_ext[:, 1:-1, 1:-1, 1:-1]
    diff_mid = diff_ext[1:-1, 1:-1, 1:-1]
    spread = jnp.zeros_like(center)
    for offset in ((1, 0, 0), (-1, 0, 0), (0, 1, 0), (0, -1, 0), (0, 0, 1), (0, 0, -1)):
        beside_conc = shifted(conc_ext, offset)
        beside_diff = shifted(diff_ext, offset)
        spread = spread + 0.5 * (diff_mid + beside_diff) * (beside_conc - center)
    drifted = jnp.zeros_like(center)
    for axis_pos in range(3):
        unit_vec = [0, 0, 0]
        unit_vec[axis_pos] = 1
        ahead = shifted(conc_ext, tuple(unit_vec))
        behind = shifted(conc_ext, tuple((-part_val for part_val in unit_vec)))
        speed_axis = ADVECT_GAIN * velocity[axis_pos]
        drifted = (
            drifted
            - jnp.maximum(speed_axis, 0.0) * (center - behind)
            - jnp.minimum(speed_axis, 0.0) * (ahead - center)
        )
    species_gain = jnp.array(DIFFUSION_GAIN, jnp.float32)[:, None, None, None]
    halfsat = jnp.array(HALF_SATURATION, jnp.float32)[:, None, None, None]
    uptake = uptake_here * center / (halfsat + jnp.abs(center))
    reaction = jnp.stack([-uptake[0], -uptake[1], 2.0 * uptake[1], -uptake[3]])
    return center + species_gain * spread + drifted + reaction


def shards(
    populations,
    viscosity,
    links,
    flags,
    neighbours,
    owners,
    slots,
    concentrations,
    diffusivity,
    uptake_rate,
):
    tables = lattice_tables()
    weights = jnp.asarray(tables["weights"], jnp.float32)
    vectors = jnp.asarray(tables["vectors"], jnp.float32)
    popul = populations[:, 0] * weights[:, None, None]
    relax = 1.0 / (3.0 * viscosity[0] + 0.5)
    link_bits = links[0]
    site_flags = flags[0]
    beside_ids = neighbours[0]
    block_count = popul.shape[1]
    request_block = jnp.take(beside_ids, jnp.asarray(tables["request_dir"], jnp.int32), axis=1)
    request_pos = jnp.asarray(tables["request_pos"], jnp.int32)
    first_block = (lax.axis_index("gx") - 1) * block_count
    local_block = request_block - first_block
    valid = (local_block >= 0) & (local_block < 3 * block_count)
    for turn_index in range(FLOW_STEPS):
        post = collide(popul, relax, vectors, weights)
        rim = rim_rows(post, tables)
        extended = padded(rim, (("gx", 0),), block_count)
        flat_index = (
            jnp.clip(local_block, 0, 3 * block_count - 1) * extended.shape[1] + request_pos[None, :]
        )
        arrived = jnp.where(valid, jnp.take(extended.reshape(-1), flat_index), 0.0)
        popul = stream(post, arrived, link_bits, beside_ids, tables)
        popul = boundary(popul, site_flags, vectors, weights)
    weighted = (popul / weights[:, None, None])[:, None]
    momentum = jnp.tensordot(vectors.T, popul, axes=1, precision=lax.Precision.HIGHEST)
    block_rows = jnp.transpose(momentum, (1, 0, 2)).reshape(block_count, 3 * 512)
    extent_x, extent_y, extent_z = concentrations.shape[1:]
    slot_x = extent_x // 8
    slot_y = extent_y // 8
    slot_z = extent_z // 8
    slot_total = slot_x * slot_y * slot_z
    owner_all = owners[0]
    slot_all = slots[0]
    my_index = lax.axis_index("gx")
    slot_ids = jnp.arange(slot_total, dtype=jnp.int32)
    start_blocks = jnp.zeros((slot_total, 3 * 512), jnp.float32)
    piece = jax.tree.map(lambda part: lax.all_gather(part, "gx", axis=0, tiled=True), block_rows)
    row_count = piece.shape[0]
    piece_owner = lax.slice_in_dim(owner_all, 0, row_count, axis=0)
    piece_slot = lax.slice_in_dim(slot_all, 0, row_count, axis=0)
    hit = (piece_owner[None, :] == my_index) & (piece_slot[None, :] == slot_ids[:, None])
    brick_blocks = start_blocks + jnp.dot(
        hit.astype(jnp.float32), piece, precision=lax.Precision.HIGHEST
    )
    velocity = (
        brick_blocks.reshape(slot_x, slot_y, slot_z, 3, 8, 8, 8)
        .transpose(3, 0, 4, 1, 5, 2, 6)
        .reshape(3, extent_x, extent_y, extent_z)
    )
    conc_ext, diff_ext = (
        padded(concentrations, (("gx", 1), ("gy", 2), ("gz", 3)), 1),
        padded(diffusivity[None], (("gx", 1), ("gy", 2), ("gz", 3)), 1),
    )
    diff_ext = diff_ext[0]
    conc = tissue_step(conc_ext, diff_ext, uptake_rate, velocity)
    for turn_index in range(TISSUE_STEPS - 1):
        conc_ext = padded(conc, (("gx", 1), ("gy", 2), ("gz", 3)), 1)
        conc = tissue_step(conc_ext, diff_ext, uptake_rate, velocity)
    return (weighted, conc)


MESH = pl.DeviceIdType.MESH
AXES = ("gx", "gy", "gz")
CHUNKS = 2


def iota(axis):
    return lax.broadcasted_iota(jnp.int32, (8, 128), axis)


def take(values, index, axis):
    return jnp.take_along_axis(values, index, axis=axis, mode="promise_in_bounds")


def swap_indices():
    row, lane = iota(0), iota(1)
    half, group, cell = lane // 64, (lane // 8) % 8, lane % 8
    ahead = half * 64 + ((group + row) % 8) * 8 + cell
    rows = (row - group + 8) % 8
    back = half * 64 + rows * 8 + cell
    return ahead, rows, back


def swap(values, indices):
    ahead, rows, back = indices
    return take(take(take(values, ahead, 1), rows, 0), back, 1)


def tables_needed():
    keys = []
    for vec in LATTICE_DIRS[1:]:
        for face_x in {0, -vec[0]}:
            for face_y in {0, -vec[1]}:
                key = (face_x, face_y, vec[2])
                if key != (0, 0, 0) and key not in keys:
                    keys.append(key)
    return sorted(keys)


TABLE_KEYS = tables_needed()


def weight_of(member):
    return 1.0 / 3.0 if member == 0 else (1.0 / 18.0 if member < 7 else 1.0 / 36.0)


def moments(popul):
    density = popul[0]
    momentum = [None, None, None]
    for member in range(1, 19):
        density = density + popul[member]
        for axis in range(3):
            sign = LATTICE_DIRS[member][axis]
            if sign:
                term = popul[member]
                if momentum[axis] is None:
                    momentum[axis] = term if sign > 0 else -term
                else:
                    momentum[axis] = momentum[axis] + term if sign > 0 else momentum[axis] - term
    return density, momentum


def relaxed(popul, density, momentum, relax):
    square = momentum[0] * momentum[0] + momentum[1] * momentum[1] + momentum[2] * momentum[2]
    rest = density - 1.5 * square
    result = [popul[0] - relax * (popul[0] - rest * (1.0 / 3.0))]
    for member in range(1, 19, 2):
        vec = LATTICE_DIRS[member]
        weight = weight_of(member)
        project = None
        for axis in range(3):
            if vec[axis]:
                term = momentum[axis]
                if project is None:
                    project = term if vec[axis] > 0 else -term
                else:
                    project = project + term if vec[axis] > 0 else project - term
        even = weight * rest + (4.5 * weight) * (project * project)
        odd = (3.0 * weight) * project
        result.append(popul[member] - relax * (popul[member] - (even + odd)))
        result.append(popul[member + 1] - relax * (popul[member + 1] - (even - odd)))
    return result


def sides_of(axis):
    count = lax.axis_size(axis)
    here = lax.axis_index(axis)
    return (
        (here > 0, {axis: lax.max(here - 1, 0)}),
        (here < count - 1, {axis: lax.min(here + 1, count - 1)}),
    )


def kernel(
    pops, visc, links, flags, beside, owners_in, slots_in, conc, diff, uptake_in,
    weighted_to, conc_to,
    weighted, conc_out, store,
    links_at, flags_at, beside_at, owners, slots, uptake, gathered, fields, post, tables, open_bits, relax_by, marks,
    cells, rates, winds, halo_x, halo_y, halo_z, pack_y, pack_z,
    load, send_g, recv_g, send_t, recv_t,
):
    count = lax.axis_size("gx")
    here = lax.axis_index("gx")
    block_count = pops.shape[1]
    species = conc.shape[0]
    planes = gathered.shape[1]
    lane, row = iota(1), iota(0)
    block_lane, cell_lane = lane // 8, lane % 8
    halos = (halo_x, halo_y, halo_z)

    pairs = (
        (pops, gathered.at[here, pl.ds(0, 19)]),
        (visc, gathered.at[here, 19]),
        (links, links_at),
        (flags, flags_at),
        (beside, beside_at),
        (conc, cells.at[0, pl.ds(0, species)]),
        (diff, cells.at[0, species]),
        (uptake_in, uptake),
        (owners_in, owners),
        (slots_in, slots),
    )
    loads = [pltpu.make_async_copy(src, dst, load.at[at]) for at, (src, dst) in enumerate(pairs)]
    for copy in loads:
        copy.start()

    for at, axis in enumerate(AXES):
        for side, (there, _) in enumerate(sides_of(axis)):

            @pl.when(jnp.logical_not(there))
            def _(at=at, side=side):
                for turn in range(TISSUE_STEPS):
                    halos[at][turn, side] = jnp.zeros(halos[at].shape[2:], jnp.float32)

    def pack(slot, turn):
        kinds = species + 1 if turn == 0 else species
        for side, spot in ((0, 0), (1, 7)):
            zcol = 0 if side == 0 else 127
            packed = jnp.zeros((8, 128), jnp.float32)
            for kind in range(kinds):
                for a in range(8):
                    tile = cells[slot, kind, a]
                    pack_y[turn, side, kind, a : a + 1] = tile[spot : spot + 1]
                    packed = jnp.where(
                        lane == kind * 8 + a,
                        jnp.broadcast_to(tile[:, zcol : zcol + 1], (8, 128)),
                        packed,
                    )
            pack_z[turn, side] = packed

    def face_copy(slot, turn, at, side, device, landing):
        kinds = species + 1 if turn == 0 else species
        if at == 0:
            source = cells.at[slot, pl.ds(0, kinds), 0 if side == 0 else 7]
            target = halo_x.at[turn, landing, pl.ds(0, kinds)]
        elif at == 1:
            source = pack_y.at[turn, side, pl.ds(0, kinds)]
            target = halo_y.at[turn, landing, pl.ds(0, kinds)]
        else:
            source = pack_z.at[turn, side]
            target = halo_z.at[turn, landing]
        return pltpu.make_async_remote_copy(
            src_ref=source,
            dst_ref=target,
            send_sem=send_t.at[turn, at * 2 + side],
            recv_sem=recv_t.at[turn, at * 2 + landing],
            device_id=device,
            device_id_type=MESH,
        )

    def start_faces(slot, turn):
        for at, axis in enumerate(AXES):
            if at == 1:
                pack(slot, turn)
            for side, (there, device) in enumerate(sides_of(axis)):

                @pl.when(there)
                def _(at=at, side=side, device=device):
                    face_copy(slot, turn, at, side, device, 1 - side).start()

    def wait_faces(slot, turn):
        for at, axis in enumerate(AXES):
            for side, (there, device) in enumerate(sides_of(axis)):

                @pl.when(there)
                def _(at=at, side=side, device=device):
                    face_copy(slot, turn, at, side, device, 1 - side).wait_send()
                    face_copy(slot, turn, at, side, device, side).wait_recv()

    barrier = pltpu.get_barrier_semaphore()
    expected = 0
    for axis in AXES:
        for there, device in sides_of(axis):

            @pl.when(there)
            def _(device=device):
                pl.semaphore_signal(barrier, inc=1, device_id=device, device_id_type=MESH)

            expected = expected + there.astype(jnp.int32)
    for copy in loads[:5]:
        copy.wait()
    gathered[here, 20] = links_at[...].astype(jnp.float32)
    gathered[here, 21] = flags_at[...].astype(jnp.float32)
    gathered[here, 22] = jnp.zeros((block_count, 512), jnp.float32)
    gathered[here, 22, :, 0:18] = beside_at[...].astype(jnp.float32)
    pl.semaphore_wait(barrier, expected)

    bounds = [0, 12, planes]
    neighbours = sides_of("gx")

    def slab_copy(owner, way, hop, part, device):
        view = gathered.at[owner, pl.ds(bounds[part], bounds[part + 1] - bounds[part])]
        return pltpu.make_async_remote_copy(
            src_ref=view,
            dst_ref=view,
            send_sem=send_g.at[way, hop, part],
            recv_sem=recv_g.at[way, hop, part],
            device_id=device,
            device_id_type=MESH,
        )

    def slab_of(way, hop):
        owner = here - hop if way == 1 else here + hop
        valid = owner >= 0 if way == 1 else owner < count
        return lax.clamp(0, owner, count - 1), valid

    indices = swap_indices()
    ahead, rows, _ = indices
    spots = [
        [half * 64 + ((row - 4 * late - block_lane % block_count + 16) % 8) * 8 + cell_lane
         for half in range(2)]
        for late in range(2)
    ]

    def absorb(owner, part, first=False):
        mine = lane // (8 * block_count) == owner

        def one(plane):
            for pair in range(2):
                both = jnp.concatenate(
                    [gathered[owner, plane, :, pl.ds((2 * pair + late) * 128, 128)]
                     for late in range(2)],
                    axis=0,
                )
                both = take(take(both, ahead, 1), rows, 0)
                for late in range(2):
                    for half in range(2):
                        a = 2 * (2 * pair + late) + half
                        moved = take(both, spots[late][half], 1)
                        if not first:
                            moved = jnp.where(mine, moved, fields[plane, a])
                        fields[plane, a] = moved

        def two(at, carry):
            one(2 * at)
            one(2 * at + 1)
            return carry

        start, end = bounds[part], min(bounds[part + 1], 22)
        lax.fori_loop(start // 2, end // 2, two, 0)

    toward = jnp.where(here >= count // 2, 1, -1)

    def absorb_at(distance, part):
        owner = here - distance * toward

        @pl.when(jnp.logical_and(owner >= 0, owner < count))
        def _():
            absorb(lax.clamp(0, owner, count - 1), part)

    for hop in range(count):
        for part in range(CHUNKS):
            for way in range(2):
                owner, valid = slab_of(way, hop)
                there, device = neighbours[way]
                back_device = neighbours[1 - way][1]
                if hop > 0:

                    @pl.when(valid)
                    def _(owner=owner, way=way, hop=hop, part=part, device=back_device):
                        slab_copy(owner, way, hop - 1, part, device).wait_recv()

                if hop < count - 1:

                    @pl.when(jnp.logical_and(valid, there))
                    def _(owner=owner, way=way, hop=hop, part=part, device=device):
                        slab_copy(owner, way, hop, part, device).start()

            if hop > 0:
                absorb_at(hop, part)

        if hop == 0:
            for copy in loads[5:]:
                copy.wait()
            start_faces(0, 0)
            for part in range(CHUNKS):
                absorb(here, part, True)
        else:
            for part in range(CHUNKS):
                if hop > 1:
                    absorb_at(1 - hop, part)
                if hop == count - 1:
                    absorb_at(-hop, part)

    for hop in range(count - 1):
        for part in range(CHUNKS):
            for way in range(2):
                owner, valid = slab_of(way, hop)
                there, device = neighbours[way]

                @pl.when(jnp.logical_and(valid, there))
                def _(owner=owner, way=way, hop=hop, part=part, device=device):
                    slab_copy(owner, way, hop, part, device).wait_send()

    low = lane < 64
    ids = jnp.concatenate([gathered[dev, 22, :, 0:128] for dev in range(4)], axis=0)
    ids = jnp.concatenate([ids, jnp.zeros((112, 128), jnp.float32)], axis=0)
    spread = lax.broadcasted_iota(jnp.int32, (128, 128), 1) // 8
    spread = (spread == lax.broadcasted_iota(jnp.int32, (128, 128), 0)).astype(jnp.float32)
    by_dir = lax.dot_general(
        ids, spread, (((0,), (0,)), ((), ())), preferred_element_type=jnp.float32
    )

    def beside_of(vec):
        at = LATTICE_DIRS.index(vec) - 1
        return jnp.broadcast_to(by_dir[at : at + 1], (8, 128)).astype(jnp.int32)

    has = {(0, 0, 0): jnp.ones((8, 128), jnp.int32)}
    for at, (face_x, face_y, step) in enumerate(TABLE_KEYS):
        inner = block_lane if face_x == 0 and face_y == 0 else beside_of((face_x, face_y, 0))
        cell = cell_lane
        if step:
            crossing = cell_lane == (0 if step > 0 else 7)
            inner = jnp.where(crossing, beside_of((face_x, face_y, -step)), inner)
            cell = (cell_lane - step + 8) % 8
        tables[at] = jnp.clip(inner, 0, 15) * 8 + cell
        has[face_x, face_y, step] = jnp.where(inner >= 0, 1, 0)

    def row_face(vec):
        return row == (0 if vec[1] > 0 else 7)

    for a in range(8):
        bits = fields[20, a].astype(jnp.int32)
        allowed = jnp.zeros((8, 128), jnp.int32)
        for member in range(1, 19):
            vec = LATTICE_DIRS[member]
            face_x = -vec[0] if not 0 <= a - vec[0] <= 7 else 0
            usable = has[face_x, 0, vec[2]]
            if vec[1]:
                usable = jnp.where(row_face(vec), has[face_x, -vec[1], vec[2]], usable)
            allowed = allowed + usable * (1 << (member - 1))
        open_bits[a] = bits & allowed
        flagged = fields[21, a]
        relax = 1.0 / (3.0 * fields[19, a] + 0.5)
        inside = flagged < 0.5
        relax_by[0, a] = jnp.where(inside, relax, 1.0)
        relax_by[1, a] = jnp.where(inside, 0.0, 1.0)
        marks[a] = jnp.where(
            inside, 0.0, jnp.where(flagged < 1.5, INLET_DENSITY, OUTLET_DENSITY)
        )

    def first_collision(a, carry):
        popul = [fields[member, a] * weight_of(member) for member in range(19)]
        density, momentum = moments(popul)
        relax = 1.0 / (3.0 * fields[19, a] + 0.5)
        for member, value in enumerate(relaxed(popul, density, momentum, relax)):
            post[0, member, a] = value
        return carry

    lax.fori_loop(0, 8, first_collision, 0)

    def flow_step(turn, carry):
        now = lax.rem(turn, 2)
        later = 1 - now
        final = jnp.where(turn == FLOW_STEPS - 1, 1, 0)
        for a in range(8):
            bits = open_bits[a]
            popul = [post[now, 0, a]]
            for member in range(1, 19):
                vec = LATTICE_DIRS[member]
                opposite = member + 1 if member % 2 else member - 1
                from_a = a - vec[0]
                face_x = 0 if 0 <= from_a <= 7 else -vec[0]
                source = post[now, member, from_a % 8]
                if vec[1]:
                    source = pltpu.roll(source, vec[1] % 8, 0)
                pulled = source
                key = (face_x, 0, vec[2])
                if key != (0, 0, 0):
                    pulled = take(source, tables[TABLE_KEYS.index(key)], 1)
                if vec[1]:
                    key = (face_x, -vec[1], vec[2])
                    other = take(source, tables[TABLE_KEYS.index(key)], 1)
                    pulled = jnp.where(row_face(vec), other, pulled)
                closed = (bits & (1 << (member - 1))) == 0
                popul.append(jnp.where(closed, post[now, opposite, a], pulled))
            density, momentum = moments(popul)
            mark = marks[a]
            density = jnp.where(mark > 0.0, mark, density)
            for member, value in enumerate(relaxed(popul, density, momentum, relax_by[final, a])):
                post[later, member, a] = value
        return carry

    lax.fori_loop(0, FLOW_STEPS, flow_step, 0)
    last = FLOW_STEPS % 2

    source_lane = jnp.full((8, 128), -1, jnp.int32)
    for block in range(16):
        owner_here = jnp.broadcast_to(owners[:, block : block + 1], (8, 128))
        slot_here = jnp.broadcast_to(slots[:, block : block + 1], (8, 128))
        hit = (owner_here == here) & (slot_here == block_lane)
        source_lane = jnp.where(hit, block * 8 + cell_lane, source_lane)
    filled = source_lane >= 0
    source_lane = jnp.maximum(source_lane, 0)
    for a in range(8):
        _, momentum = moments([post[last, member, a] for member in range(19)])
        for axis in range(3):
            speed = ADVECT_GAIN * jnp.where(filled, take(momentum[axis], source_lane, 1), 0.0)
            winds[2 * axis, a] = jnp.maximum(speed, 0.0)
            winds[2 * axis + 1, a] = -jnp.minimum(speed, 0.0)

    def beside_cells(slot, turn, kind, a):
        center = cells[slot, kind, a]
        result = []
        result.append(halo_x[turn, 0, kind] if a == 0 else cells[slot, kind, a - 1])
        result.append(halo_x[turn, 1, kind] if a == 7 else cells[slot, kind, a + 1])
        for side, spot in ((0, 0), (1, 7)):
            edge = jnp.broadcast_to(halo_y[turn, side, kind, a : a + 1], (8, 128))
            result.append(jnp.where(row == spot, edge, pltpu.roll(center, 1 if side == 0 else 7, 0)))
        for side, spot in ((0, 0), (1, 127)):
            col = kind * 8 + a
            edge = jnp.broadcast_to(halo_z[turn, side, :, col : col + 1], (8, 128))
            result.append(jnp.where(lane == spot, edge, pltpu.roll(center, 1 if side == 0 else 127, 1)))
        return center, result

    def tissue(slot, turn):
        for a in range(8):
            if turn == 0:
                center, around = beside_cells(0, 0, species, a)
                for way in range(6):
                    rates[way, a] = 0.5 * (center + around[way])
            rate = [rates[way, a] for way in range(6)]
            wind = [winds[way, a] for way in range(6)]
            appetite = uptake[a]
            eaten = None
            for kind in range(species):
                center, around = beside_cells(slot, turn, kind, a)
                total = center
                for way in range(6):
                    gain = DIFFUSION_GAIN[kind] * rate[way] + wind[way]
                    total = total + gain * (around[way] - center)
                if kind != 2:
                    eaten_here = appetite * center / (HALF_SATURATION[kind] + jnp.abs(center))
                    total = total - eaten_here
                    if kind == 1:
                        eaten = eaten_here
                else:
                    total = total + 2.0 * eaten
                if turn == TISSUE_STEPS - 1:
                    conc_out[kind, a] = total
                else:
                    cells[1 - slot, kind, a] = total
            if turn == TISSUE_STEPS - 1 and a % 4 == 3:
                conc_copies[a // 4].start()

    upper = here * block_count >= 8
    shift_rows = lax.rem(here * block_count, 8) > 0

    def hand_out_one(member):
        scale = jnp.where(jnp.asarray(member) == 0, 3.0, jnp.where(jnp.asarray(member) < 7, 18.0, 36.0))
        for tile in range(4):
            even = post[last, member, 2 * tile]
            odd = post[last, member, 2 * tile + 1]
            lower_part = jnp.where(low, even, pltpu.roll(odd, 64, 1))
            upper_part = jnp.where(low, pltpu.roll(even, 64, 1), odd)
            rows = swap(jnp.where(upper, upper_part, lower_part), indices) * scale
            rows = jnp.where(shift_rows, pltpu.roll(rows, 4, 0), rows)
            weighted[member, :, pl.ds(tile * 128, 128)] = rows[0:4]

    def hand_out(first, end):
        def three(at, carry):
            for more in range(3):
                hand_out_one(first + 3 * at + more)
            return carry

        lax.fori_loop(0, (end - first) // 3, three, 0)
        for member in range(end - (end - first) % 3, end):
            hand_out_one(member)

    weighted_copy = pltpu.make_async_copy(weighted, weighted_to, store.at[2])
    conc_copies = []
    for part in range(2):
        cut = pl.ds(4 * part, 4)
        conc_copies.append(
            pltpu.make_async_copy(conc_out.at[:, cut], conc_to.at[:, cut], store.at[part])
        )

    for turn in range(TISSUE_STEPS):
        slot = turn % 2
        if turn > 0:
            start_faces(slot, turn)
            first = 19 * (turn - 1) // (TISSUE_STEPS - 1)
            hand_out(first, 19 * turn // (TISSUE_STEPS - 1))
        if turn == TISSUE_STEPS - 1:
            weighted_copy.start()
        wait_faces(slot, turn)
        tissue(slot, turn)
    for copy in conc_copies:
        copy.wait()
    weighted_copy.wait()


def fused(
    populations, viscosity, links, flags, neighbours, owners, slots,
    concentrations, diffusivity, uptake_rate,
):
    count = lax.axis_size("gx")
    block_count = populations.shape[2]
    species = concentrations.shape[0]
    hbm = pl.BlockSpec(memory_space=pltpu.HBM)
    f32 = jnp.float32
    weighted, conc = pl.pallas_call(
        kernel,
        out_shape=(
            jax.ShapeDtypeStruct((19, block_count, 512), f32),
            jax.ShapeDtypeStruct(concentrations.shape, f32),
        ),
        in_specs=[hbm] * 10,
        out_specs=(hbm, hbm),
        scratch_shapes=[
            pltpu.VMEM((19, block_count, 512), f32),
            pltpu.VMEM(concentrations.shape, f32),
            pltpu.SemaphoreType.DMA((3,)),
            pltpu.VMEM((block_count, 512), jnp.int32),
            pltpu.VMEM((block_count, 512), jnp.int32),
            pltpu.VMEM((block_count, 18), jnp.int32),
            pltpu.VMEM(owners.shape, jnp.int32),
            pltpu.VMEM(slots.shape, jnp.int32),
            pltpu.VMEM(uptake_rate.shape, f32),
            pltpu.VMEM((count, 23, block_count, 512), f32),
            pltpu.VMEM((22, 8, 8, 128), f32),
            pltpu.VMEM((2, 19, 8, 8, 128), f32),
            pltpu.VMEM((len(TABLE_KEYS), 8, 128), jnp.int32),
            pltpu.VMEM((8, 8, 128), jnp.int32),
            pltpu.VMEM((2, 8, 8, 128), f32),
            pltpu.VMEM((8, 8, 128), f32),
            pltpu.VMEM((2, species + 1, 8, 8, 128), f32),
            pltpu.VMEM((6, 8, 8, 128), f32),
            pltpu.VMEM((6, 8, 8, 128), f32),
            pltpu.VMEM((TISSUE_STEPS, 2, species + 1, 8, 128), f32),
            pltpu.VMEM((TISSUE_STEPS, 2, species + 1, 8, 128), f32),
            pltpu.VMEM((TISSUE_STEPS, 2, 8, 128), f32),
            pltpu.VMEM((TISSUE_STEPS, 2, species + 1, 8, 128), f32),
            pltpu.VMEM((TISSUE_STEPS, 2, 8, 128), f32),
            pltpu.SemaphoreType.DMA((10,)),
            pltpu.SemaphoreType.DMA((2, count - 1, CHUNKS)),
            pltpu.SemaphoreType.DMA((2, count - 1, CHUNKS)),
            pltpu.SemaphoreType.DMA((TISSUE_STEPS, 6)),
            pltpu.SemaphoreType.DMA((TISSUE_STEPS, 6)),
        ],
        compiler_params=pltpu.CompilerParams(
            collective_id=0, has_side_effects=True, vmem_limit_bytes=64 * 1024 * 1024
        ),
    )(
        populations[:, 0], viscosity[0], links[0], flags[0], neighbours[0], owners, slots,
        concentrations, diffusivity, uptake_rate,
    )
    return weighted[:, None], conc


def per_device(*arrays):
    populations, concentrations = arrays[0], arrays[7]
    fits = (
        lax.axis_size("gx") == 4
        and populations.shape[2] == 4
        and concentrations.shape[1:] == (8, 8, 128)
    )
    return fused(*arrays) if fits else shards(*arrays)


def solution(mesh):
    return jax.shard_map(
        per_device,
        mesh=mesh,
        in_specs=(
            P(None, ("gy", "gz"), "gx", None),
            P(("gy", "gz"), "gx", None),
            P(("gy", "gz"), "gx", None),
            P(("gy", "gz"), "gx", None),
            P(("gy", "gz"), "gx", None),
            P(("gy", "gz"), None),
            P(("gy", "gz"), None),
            P(None, "gx", "gy", "gz"),
            P("gx", "gy", "gz"),
            P("gx", "gy", "gz"),
        ),
        out_specs=(P(None, ("gy", "gz"), "gx", None), P(None, "gx", "gy", "gz")),
        check_vma=False,
    )
```
